32 devices in a mesh: req: 8 (over z, x), kv: 4 (over y, core).
Axes of the slice: x: 2, y: 2, z: 4, core: 2. Of those that a mesh axis runs over, the one named last changes fastest.
Arguments:
- hidden: bfloat16 [32, 5120], P('kv', 'req'), may hold values from -120 to 120
- gain: bfloat16 [5120], P('req'), may hold values from 0.5 to 1.5
- w_query: bfloat16 [5120, 5120], P('req', 'kv'), may hold values from -0.078125 to 0.078125
- w_key: bfloat16 [5120, 1024], P('req', 'kv'), may hold values from -0.078125 to 0.078125
- w_value: bfloat16 [5120, 1024], P('req', 'kv'), may hold values from -0.078125 to 0.078125
- b_query: bfloat16 [5120], P('kv'), may hold values from -3 to 3
- b_key: bfloat16 [1024], P('kv'), may hold values from -3 to 3
- b_value: bfloat16 [1024], P('kv'), may hold values from -3 to 3
- w_output: bfloat16 [5120, 5120], P('kv', 'req'), may hold values from -0.5 to 0.5
- key_cache: bfloat16 [32, 8, 4096, 128], P('req', 'kv'), may hold values from -160 to 160
- value_cache: bfloat16 [32, 8, 4096, 128], P('req', 'kv'), may hold values from -9 to 9
- sink_keys: bfloat16 [32, 8, 4, 128], P('req', 'kv'), may hold values from -6 to 6
- sink_values: bfloat16 [32, 8, 4, 128], P('req', 'kv'), may hold values from -9 to 9
- lengths: int32 [32], P('req'), may hold values from 4 to 8192, as said below
- sink_count: int32 [32], P('req'), may hold values from 0 to 4, as said below
- window: int32 [32], P('req'), may hold values from 1024 to 4096, as said below
Outputs:
- attn_out: bfloat16 [32, 5120], P('kv', 'req')
The draws below stay inside these ranges and needn't reach their ends.
Inputs may be any that keep to these rules, and one draw needn't show every extreme that they name: `lengths`: exactly 2 requests have length 8192; the others are heavy-tailed below it. `sink_count`: some request keeps 4. Some request has window 4096.
All inputs are finite; a program needn't handle non-finite values.
Results may differ from the reference program's by a relative error of at most 0.012.
The reference program's roundings to bfloat16 on the way count: a program that leaves them out, or rounds other values in their place, can miss the bound.
Values may be sent and summed in bfloat16 or wider, within the bound.
No kernel may reach another device: no remote copies, remote signals or barrier semaphores. Data moves between devices by JAX's collectives and lax.ppermute only.
A program may use at most 64 MiB of HBM per device.

```python
import math
import jax
import jax.numpy as jnp
from jax import lax

D = 5120
HQ = 40
KVH = 8
HD = 128
GROUP = 5
REQUESTS = 32
CYCLE = 4096
SINKS = 4
MAXLEN = 8192
LONGS = 2


def draw_hidden(key, part):
    first = jax.random.fold_in(key, 0)
    ramp = jnp.exp(math.log(3.0) * jnp.arange(D, dtype=jnp.float32) / D)
    base = jnp.clip(jax.random.normal(first, (REQUESTS, D), jnp.float32), -4.0, 4.0)
    return (base * ramp[None, :]).astype(jnp.bfloat16)


def draw_key_cache(key, part):
    first = jax.random.fold_in(key, 0)
    shape = (REQUESTS, KVH, CYCLE, HD)
    base = jnp.clip(jax.random.normal(first, shape, jnp.float32), -5.0, 5.0)
    return base.astype(jnp.bfloat16)


def draw_lengths(key, part):
    first, second, third = jax.random.split(key, 3)
    top_bit = MAXLEN.bit_length() - 1
    exponent = jax.random.randint(first, (REQUESTS,), 2, top_bit)
    base = jnp.left_shift(jnp.ones((REQUESTS,), jnp.int32), exponent)
    extra = jax.random.randint(second, (REQUESTS,), 0, base)
    result = base + extra
    order = jax.random.permutation(third, REQUESTS)
    return result.at[order[:LONGS]].set(MAXLEN).astype(jnp.int32)


def draw_sink_count(key, part):
    first, second = jax.random.split(jax.random.fold_in(key, 11))
    result = jax.random.randint(first, (REQUESTS,), 0, SINKS + 1)
    where_full = jax.random.randint(second, (), 0, REQUESTS)
    return result.at[where_full].set(SINKS).astype(jnp.int32)


def draw_window(key, part):
    first, second = jax.random.split(jax.random.fold_in(key, 23))
    result = jax.random.randint(first, (REQUESTS,), CYCLE // 4, CYCLE + 1)
    where_full = jax.random.randint(second, (), 0, REQUESTS)
    return result.at[where_full].set(CYCLE).astype(jnp.int32)


def level_of(key, shape, cuts, least, top_value):
    level, own = 1.0, jax.random.fold_in(key, 6)
    for dim, blocks in cuts:
        draws = jnp.exp(jax.random.uniform(jax.random.fold_in(own, dim), (blocks,), jnp.float32, least / len(cuts), top_value / len(cuts)))
        level = level * jnp.repeat(draws, shape[dim] // blocks).reshape([-1 if axis == dim else 1 for axis in range(len(shape))])
    return level


def scatter_about(key, dims, width, most, pieces=(), kind=jnp.bfloat16):
    drawn = jax.random.normal(key, dims, jnp.float32) * width
    if len(pieces) > 0:
        drawn = level_of(key, dims, pieces, -0.22, 0.18) * drawn
    return jnp.clip(drawn, min=-most, max=most).astype(kind)


def setup_inputs(seed: int = 0) -> dict:
    splits = jax.random.split(jax.random.key(seed), 17)
    hidden = draw_hidden(jax.random.fold_in(splits[16], 71), 0)
    gain = jnp.clip(1.0 + 0.1 * jax.random.normal(splits[1], (D,), jnp.float32), 0.5, 1.5).astype(jnp.bfloat16)
    w_query = scatter_about(splits[2], (D, HQ * HD), D ** -0.5, 0.078125, ((0, 8), (1, 4)))
    w_key = scatter_about(splits[3], (D, KVH * HD), D ** -0.5, 0.078125, ((0, 8), (1, 4)))
    w_value = scatter_about(splits[4], (D, KVH * HD), D ** -0.5, 0.078125, ((0, 8), (1, 4)))
    b_query = scatter_about(splits[5], (HQ * HD,), 0.5, 3.0, ((0, 4),))
    b_key = scatter_about(splits[6], (KVH * HD,), 0.5, 3.0, ((0, 4),))
    b_value = scatter_about(splits[7], (KVH * HD,), 0.5, 3.0, ((0, 4),))
    w_output = scatter_about(splits[8], (HQ * HD, D), HD ** -0.5, 0.5, ((0, 4), (1, 8)))
    key_cache = draw_key_cache(jax.random.fold_in(splits[16], 71), 0)
    value_cache = scatter_about(splits[10], (REQUESTS, KVH, CYCLE, HD), 1.5, 9.0, ((0, 8), (1, 4)))
    sink_keys = scatter_about(splits[11], (REQUESTS, KVH, SINKS, HD), 1.0, 6.0, ((0, 8), (1, 4)))
    sink_values = scatter_about(splits[12], (REQUESTS, KVH, SINKS, HD), 1.5, 9.0, ((0, 8), (1, 4)))
    lengths = draw_lengths(jax.random.fold_in(splits[16], 71), 0)
    sink_count = draw_sink_count(jax.random.fold_in(splits[16], 71), 0)
    window = draw_window(jax.random.fold_in(splits[16], 71), 0)
    return {"hidden": hidden, "gain": gain, "w_query": w_query, "w_key": w_key, "w_value": w_value, "b_query": b_query, "b_key": b_key, "b_value": b_value, "w_output": w_output, "key_cache": key_cache, "value_cache": value_cache, "sink_keys": sink_keys, "sink_values": sink_values, "lengths": lengths, "sink_count": sink_count, "window": window}


def rotate(window_values, positions):
    half = window_values.shape[-1] // 2
    freq = jnp.power(1000000.0, -2.0 * jnp.arange(half, dtype=jnp.float32) / window_values.shape[-1])
    angle = positions[..., None] * freq
    cosine = jnp.cos(angle)
    sine = jnp.sin(angle)
    first = window_values[..., :half]
    second = window_values[..., half:]
    return jnp.concatenate([first * cosine - second * sine, second * cosine + first * sine], -1)

def attend(entry_list):
    query_vector, fresh_key, fresh_value, window_keys, window_values, anchor_keys, anchor_values, cache_length, sink_tokens, window = entry_list
    score_scale = 1.0 / math.sqrt(HD)
    query_float = query_vector.astype(jnp.float32)
    s_cache = jnp.einsum('zni,zxi->znx', query_float, window_keys.astype(jnp.float32)) * score_scale
    sink_score = jnp.einsum('zni,zxi->znx', query_float, anchor_keys.astype(jnp.float32)) * score_scale
    s_self = lax.optimization_barrier(jnp.sum(query_float * fresh_key.astype(jnp.float32)[:, None, :], -1)) * score_scale
    slot = jnp.arange(CYCLE, dtype=jnp.int32)
    place = slot + CYCLE * ((cache_length - 1 - slot) // CYCLE)
    live_cache = (slot < cache_length) & (place >= jnp.maximum(sink_tokens, cache_length - window))
    live_sink = jnp.arange(SINKS, dtype=jnp.int32) < jnp.minimum(sink_tokens, cache_length)
    top = jnp.maximum(lax.optimization_barrier(jnp.max(jnp.where(live_cache, s_cache, -jnp.inf), -1)), lax.optimization_barrier(jnp.max(jnp.where(live_sink, sink_score, -jnp.inf), -1)))
    top = jnp.maximum(top, s_self)
    e_cache = jnp.where(live_cache, jnp.exp(s_cache - top[..., None]), 0.0)
    e_sink = jnp.where(live_sink, jnp.exp(sink_score - top[..., None]), 0.0)
    e_self = jnp.exp(s_self - top)
    total = lax.optimization_barrier(jnp.sum(e_cache, -1)) + lax.optimization_barrier(jnp.sum(e_sink, -1)) + e_self
    numer = jnp.einsum('kgs,ksd->kgd', e_cache.astype(jnp.bfloat16).astype(jnp.float32), window_values.astype(jnp.float32))
    numer = numer + jnp.einsum('kgs,ksd->kgd', e_sink.astype(jnp.bfloat16).astype(jnp.float32), anchor_values.astype(jnp.float32))
    numer = numer + e_self.astype(jnp.bfloat16).astype(jnp.float32)[..., None] * fresh_value.astype(jnp.float32)[:, None, :]
    return (numer / total[..., None]).astype(jnp.bfloat16)

def reference(hidden, gain, w_query, w_key, w_value, b_query, b_key, b_value, w_output, key_cache, value_cache, sink_keys, sink_values, lengths, sink_count, window):
    xf = hidden.astype(jnp.float32)
    inv_rms = lax.rsqrt(lax.optimization_barrier(jnp.sum(xf * xf, 1)) / D + 1e-06)
    scaled = (xf * gain.astype(jnp.float32)).astype(jnp.bfloat16)
    query_vector = inv_rms[:, None] * jnp.dot(scaled, w_query, preferred_element_type=jnp.float32) + b_query.astype(jnp.float32)
    fresh_key = inv_rms[:, None] * jnp.dot(scaled, w_key, preferred_element_type=jnp.float32) + b_key.astype(jnp.float32)
    value_f = inv_rms[:, None] * jnp.dot(scaled, w_value, preferred_element_type=jnp.float32) + b_value.astype(jnp.float32)
    positions = lengths.astype(jnp.float32)[:, None]
    q_rot = rotate(query_vector.reshape(REQUESTS, HQ, HD), positions).astype(jnp.bfloat16).reshape(REQUESTS, KVH, GROUP, HD)
    k_rot = rotate(fresh_key.reshape(REQUESTS, KVH, HD), positions).astype(jnp.bfloat16)
    fresh_value = value_f.reshape(REQUESTS, KVH, HD).astype(jnp.bfloat16)
    context = lax.map(attend, (q_rot, k_rot, fresh_value, key_cache, value_cache, sink_keys, sink_values, lengths, sink_count, window))
    context = context.reshape(REQUESTS, HQ * HD)
    return jnp.dot(context, w_output, preferred_element_type=jnp.float32).astype(jnp.bfloat16)
```

```python
import math

import jax
import jax.numpy as jnp
from jax import lax
from jax.experimental import pallas as pl
from jax.experimental.pallas import tpu as pltpu
from jax.sharding import PartitionSpec as P

D = 5120
SINKS = 4
EPS = 1e-06
BLOCK = 512
EXTRA = 128


def log2(n):
    bits = n.bit_length() - 1
    assert n == 1 << bits
    return bits


def stages(n):
    bits = log2(n)
    if bits == 0:
        return []
    result = [(2, 1)]
    left = bits - 1
    while left:
        take = 2 if left % 2 == 0 else 1
        left -= take
        result.append((1 << take, 2 << left))
    return result


def place_to_offset(place, n):
    bits = log2(n)
    if bits == 0:
        return place
    return ((place << 1) | (place >> (bits - 1))) & (n - 1)


def offset_to_place(offset, n):
    bits = log2(n)
    if bits == 0:
        return offset
    return (offset >> 1) | ((offset & 1) << (bits - 1))


def swap(x, axis, n, offset):
    return lax.ppermute(x, axis, [(i, i ^ offset) for i in range(n)])


def gather_blocks(x, axis, n):
    for radix, unit in reversed(stages(n)):
        x = jnp.concatenate([x] + [swap(x, axis, n, q * unit) for q in range(1, radix)], 0)
    return x


def row_order(size, rows_req, rows_kv, req, kv, to_kv):
    n_req, n_kv = size // rows_req, size // rows_kv
    shape = (size, size)
    req_row = lax.broadcasted_iota(jnp.int32, shape, 1 if to_kv else 0)
    kv_row = lax.broadcasted_iota(jnp.int32, shape, 0 if to_kv else 1)
    place = req_row >> log2(rows_req)
    owner = place_to_offset(place, n_req) ^ req
    request = (owner << log2(rows_req)) | (req_row & (rows_req - 1))
    kv_place = offset_to_place((request >> log2(rows_kv)) ^ kv, n_kv)
    kv_request = (kv_place << log2(rows_kv)) | (request & (rows_kv - 1))
    return (kv_request == kv_row).astype(jnp.bfloat16)


def project_kernel(rows_req, hidden, gain, w_query, w_key, w_value, keep, send):
    size = hidden.shape[0]
    rows_kv = size // lax.axis_size("kv")
    order = row_order(
        size, rows_req, rows_kv, lax.axis_index("req"), lax.axis_index("kv"), False
    )
    xf = jnp.dot(order, hidden[...], preferred_element_type=jnp.float32)
    scaled = (xf * gain[...].astype(jnp.float32)).astype(jnp.bfloat16)
    half = keep.shape[0]

    def put(start, block):
        width = block.shape[1]
        keep[:, start : start + width] = block[:half]
        send[:, start : start + width] = block[half:]

    at = 0
    for weight in (w_query, w_key, w_value):
        put(at, jnp.dot(scaled, weight[...], preferred_element_type=jnp.float32))
        at += weight.shape[1]
    squares = jnp.sum(xf * xf, 1, keepdims=True)
    put(at, jnp.broadcast_to(squares, (size, EXTRA)))


def attend_kernel(
    n_parts,
    lengths,
    sink_count,
    window,
    *refs,
):
    parts = refs[:n_parts]
    (
        cosine,
        sine,
        b_query,
        b_key,
        b_value,
        key_cache,
        value_cache,
        sink_keys,
        sink_values,
        context,
        k_buf,
        v_buf,
        score_buf,
        q_heads,
        k_extra,
        v_extra,
        k_sem,
        v_sem,
    ) = refs[n_parts:]
    count, heads_kv, cycle, size = key_cache.shape
    group = context.shape[1] // (heads_kv * size)
    pad = q_heads.shape[1] // heads_kv
    blocks = cycle // BLOCK
    scale = 1.0 / math.sqrt(size)

    def span(r):
        low = jnp.maximum(sink_count[r], lengths[r] - window[r])
        first = low // BLOCK
        visits = (lengths[r] - 1) // BLOCK - first + 1
        return low, first, jnp.maximum(visits, 0)

    spans = [span(r) for r in range(count)]

    def copy(cache, buf, sem, r, t):
        at = lax.rem(spans[r][1] + t, blocks)
        src = pl.ds(pl.multiple_of(at * BLOCK, BLOCK), BLOCK)
        dst = pl.ds(pl.multiple_of(t * BLOCK, BLOCK), BLOCK)
        return pltpu.make_async_copy(cache.at[r, :, src], buf.at[r, :, dst], sem.at[r, t])

    keys = (key_cache, k_buf, k_sem)
    values = (value_cache, v_buf, v_sem)
    for which in (keys, values):
        for r in range(count):

            @pl.loop(0, spans[r][2])
            def _(t):
                copy(*which, r, t).start()

    total = parts[0][...]
    for part in parts[1:]:
        total = total + part[...]
    q_cols, kv_cols = b_query.shape[1], b_key.shape[1]
    squares = total[:, q_cols + 2 * kv_cols : q_cols + 2 * kv_cols + 1]
    inv_rms = lax.rsqrt(squares / D + EPS)
    query = inv_rms * total[:, :q_cols] + b_query[...].astype(jnp.float32)
    key = inv_rms * total[:, q_cols : q_cols + kv_cols] + b_key[...].astype(jnp.float32)
    value = inv_rms * total[:, q_cols + kv_cols : q_cols + 2 * kv_cols] + b_value[...].astype(
        jnp.float32
    )
    cos, sin = cosine[...], sine[...]

    def rotated(x):
        return x * cos + pltpu.roll(x, size // 2, 1) * sin

    q_heads[...] = jnp.zeros_like(q_heads)
    k_extra[...] = jnp.zeros_like(k_extra)
    v_extra[...] = jnp.zeros_like(v_extra)
    for h in range(heads_kv):
        lanes = slice(h * size, (h + 1) * size)
        for g in range(group):
            head = h * group + g
            block = rotated(query[:, head * size : (head + 1) * size])
            for r in range(count):
                q_heads[r, h * pad + g : h * pad + g + 1, lanes] = block[r : r + 1]
        k_rot = rotated(key[:, lanes])
        for r in range(count):
            k_extra[r, 0:SINKS, lanes] = sink_keys[r, h].astype(jnp.float32)
            v_extra[r, 0:SINKS, lanes] = sink_values[r, h].astype(jnp.float32)
            k_extra[r, SINKS : SINKS + 1, lanes] = k_rot[r : r + 1]
            v_extra[r, SINKS : SINKS + 1, lanes] = value[r : r + 1, lanes]

    contract_last = (((1,), (1,)), ((), ()))
    lane = lax.broadcasted_iota(jnp.int32, (1, EXTRA), 1)
    offset = lax.broadcasted_iota(jnp.int32, (1, BLOCK), 1)
    for r in range(count):
        length = lengths[r]
        low, first, visits = spans[r]
        q = q_heads[r].astype(jnp.bfloat16)
        extra = (
            lax.dot_general(
                q,
                k_extra[r].astype(jnp.bfloat16),
                contract_last,
                preferred_element_type=jnp.float32,
            )
            * scale
        )
        live = (lane < jnp.minimum(sink_count[r], length)) | (lane == SINKS)
        extra = jnp.where(live, extra, -jnp.inf)

        def both(buf, t):
            rows = pl.ds(pl.multiple_of(t * BLOCK, BLOCK), BLOCK)
            return jnp.concatenate([buf[r, h, rows] for h in range(heads_kv)], 1)

        def score(t, top):
            copy(*keys, r, t).wait()
            s = (
                lax.dot_general(
                    q, both(k_buf, t), contract_last, preferred_element_type=jnp.float32
                )
                * scale
            )
            position = (first + t) * BLOCK + offset
            s = jnp.where((position >= low) & (position < length), s, -jnp.inf)
            score_buf[t] = s
            return jnp.maximum(top, jnp.max(s, 1, keepdims=True))

        top = lax.fori_loop(0, visits, score, jnp.max(extra, 1, keepdims=True))
        weights = jnp.exp(extra - top)
        denom = jnp.sum(weights, 1, keepdims=True)
        numer = jnp.dot(
            weights.astype(jnp.bfloat16),
            v_extra[r].astype(jnp.bfloat16),
            preferred_element_type=jnp.float32,
        )

        def mix(t, carry):
            denom, numer = carry
            copy(*values, r, t).wait()
            weights = jnp.exp(score_buf[t] - top)
            denom = denom + jnp.sum(weights, 1, keepdims=True)
            numer = numer + jnp.dot(
                weights.astype(jnp.bfloat16), both(v_buf, t), preferred_element_type=jnp.float32
            )
            return denom, numer

        denom, numer = lax.fori_loop(0, visits, mix, (denom, numer))
        result = (numer / denom).astype(jnp.bfloat16).astype(jnp.float32)
        for h in range(heads_kv):
            for g in range(group):
                head = h * group + g
                context[r : r + 1, head * size : (head + 1) * size] = result[
                    h * pad + g : h * pad + g + 1, h * size : (h + 1) * size
                ]


def output_kernel(rows_kv, context, w_output, keep, send):
    size = context.shape[0]
    rows_req = size // lax.axis_size("req")
    order = row_order(
        size, rows_req, rows_kv, lax.axis_index("req"), lax.axis_index("kv"), True
    )
    rows = jnp.dot(order, context[...], preferred_element_type=jnp.float32).astype(jnp.bfloat16)
    product = jnp.dot(rows, w_output[...], preferred_element_type=jnp.float32)
    half = keep.shape[0]
    keep[...] = product[:half]
    send[...] = product[half:]


def spec(space=pltpu.VMEM):
    return pl.BlockSpec(memory_space=space)


def on_device(
    hidden,
    gain,
    w_query,
    w_key,
    w_value,
    b_query,
    b_key,
    b_value,
    w_output,
    key_cache,
    value_cache,
    sink_keys,
    sink_values,
    lengths,
    sink_count,
    window,
):
    n_req, n_kv = lax.axis_size("req"), lax.axis_size("kv")
    count, heads_kv, cycle, size = key_cache.shape
    rows_kv = hidden.shape[0]
    rows = count * n_req
    q_cols, kv_cols = w_query.shape[1], w_key.shape[1]
    group = q_cols // (heads_kv * size)
    wide = q_cols + 2 * kv_cols + EXTRA
    f32, bf16 = jnp.float32, jnp.bfloat16

    gathered = gather_blocks(hidden, "kv", n_kv)
    half = jax.ShapeDtypeStruct((rows // 2, wide), f32)
    keep, send = pl.pallas_call(
        lambda *refs: project_kernel(count, *refs),
        out_shape=(half, half),
        in_specs=[spec()] * 5,
        out_specs=(spec(), spec()),
        compiler_params=pltpu.CompilerParams(vmem_limit_bytes=16 << 20),
        name="project",
    )(gathered, gain.reshape(1, -1), w_query, w_key, w_value)

    req_stages = stages(n_req)
    received = swap(send, "req", n_req, req_stages[0][1])
    parts = [keep, received]
    for radix, unit in req_stages[1:]:
        x = sum(parts[1:], parts[0])
        chunk = x.shape[0] // radix
        parts = [x[:chunk]] + [
            swap(x[q * chunk : (q + 1) * chunk], "req", n_req, q * unit) for q in range(1, radix)
        ]

    freq = jnp.power(1000000.0, -2.0 * jnp.arange(size // 2, dtype=f32) / size)
    angle = lengths.astype(f32)[:, None] * freq
    cos, sin = jnp.cos(angle), jnp.sin(angle)
    cosine = jnp.concatenate([cos, cos], 1)
    sine = jnp.concatenate([-sin, sin], 1)

    visits = cycle // BLOCK + 1
    pad = -(-group // 8) * 8
    stored = visits * BLOCK
    context = pl.pallas_call(
        lambda *refs: attend_kernel(len(parts), *refs),
        out_shape=jax.ShapeDtypeStruct((count, q_cols), f32),
        in_specs=[spec(pltpu.SMEM)] * 3
        + [spec()] * (len(parts) + 5)
        + [spec(pl.ANY)] * 2
        + [spec()] * 2,
        out_specs=spec(),
        scratch_shapes=[
            pltpu.VMEM((count, heads_kv, stored, size), bf16),
            pltpu.VMEM((count, heads_kv, stored, size), bf16),
            pltpu.VMEM((visits, heads_kv * pad, BLOCK), f32),
            pltpu.VMEM((count, heads_kv * pad, heads_kv * size), f32),
            pltpu.VMEM((count, EXTRA, heads_kv * size), f32),
            pltpu.VMEM((count, EXTRA, heads_kv * size), f32),
            pltpu.SemaphoreType.DMA((count, visits)),
            pltpu.SemaphoreType.DMA((count, visits)),
        ],
        compiler_params=pltpu.CompilerParams(vmem_limit_bytes=32 << 20),
        name="attend",
    )(
        lengths,
        sink_count,
        window,
        *parts,
        cosine,
        sine,
        b_query.reshape(1, -1),
        b_key.reshape(1, -1),
        b_value.reshape(1, -1),
        key_cache,
        value_cache,
        sink_keys,
        sink_values,
    ).astype(bf16)

    everyone = gather_blocks(context, "req", n_req)
    half = jax.ShapeDtypeStruct((rows // 2, w_output.shape[1]), f32)
    keep, send = pl.pallas_call(
        lambda *refs: output_kernel(rows_kv, *refs),
        out_shape=(half, half),
        in_specs=[spec()] * 2,
        out_specs=(spec(), spec()),
        compiler_params=pltpu.CompilerParams(vmem_limit_bytes=16 << 20),
        name="output",
    )(everyone, w_output)
    kv_stages = stages(n_kv)
    x = keep + swap(send, "kv", n_kv, kv_stages[0][1])
    for radix, unit in kv_stages[1:]:
        chunk = x.shape[0] // radix
        parts = [x[:chunk]] + [
            swap(x[q * chunk : (q + 1) * chunk], "kv", n_kv, q * unit) for q in range(1, radix)
        ]
        x = sum(parts[1:], parts[0])
    return x.astype(bf16)


def solution(mesh):
    in_specs = (
        P("kv", "req"),
        P("req"),
        P("req", "kv"),
        P("req", "kv"),
        P("req", "kv"),
        P("kv"),
        P("kv"),
        P("kv"),
        P("kv", "req"),
        P("req", "kv", None, None),
        P("req", "kv", None, None),
        P("req", "kv", None, None),
        P("req", "kv", None, None),
        P("req"),
        P("req"),
        P("req"),
    )
    out_specs = P("kv", "req")
    return jax.shard_map(
        on_device, mesh=mesh, in_specs=in_specs, out_specs=out_specs, check_vma=False
    )
```

```python
import math

import jax
import jax.numpy as jnp
from jax import lax
from jax.experimental import pallas as pl
from jax.experimental.pallas import tpu as pltpu
from jax.sharding import PartitionSpec as P

D = 5120
SINKS = 4
EPS = 1e-06
BLOCK = 512
PLAN_BITS = 4
TOGETHER = 4
LANES = 128
STAGE_BITS = 2

EXTRA_ROWS = 16


def log2(n):
    bits = n.bit_length() - 1
    assert n == 1 << bits
    return bits


def stages(n, most):
    bits = log2(n)
    if bits == 0:
        return []
    result = [(2, 1)]
    left = bits - 1
    while left:
        take = most if left % most == 0 else 1
        left -= take
        result.append((1 << take, 2 << left))
    return result


def crossed(offset, kv):
    low = offset & 3
    turned = ((low & 1) << 1) | (low >> 1)
    return offset ^ ((low ^ turned) * (kv & 1))


def place_to_offset(place, n):
    bits = log2(n)
    if bits == 0:
        return place
    return ((place << 1) | (place >> (bits - 1))) & (n - 1)


def swap_req(x, n_req, n_kv, offset):
    pairs = [
        (i * n_kv + j, (i ^ (crossed(offset, j) if n_req > 2 else offset)) * n_kv + j)
        for i in range(n_req)
        for j in range(n_kv)
    ]
    return lax.ppermute(x, ("req", "kv"), pairs)


def swap_kv(x, n_kv, offset):
    return lax.ppermute(x, "kv", [(j, j ^ offset) for j in range(n_kv)])


def row_order(size, rows_req, rows_kv, to_kv):
    req, kv = lax.axis_index("req"), lax.axis_index("kv")
    n_req = size // rows_req
    shape = (size, size)
    req_row = lax.broadcasted_iota(jnp.int32, shape, 1 if to_kv else 0)
    kv_row = lax.broadcasted_iota(jnp.int32, shape, 0 if to_kv else 1)
    offset = place_to_offset(req_row >> log2(rows_req), n_req)
    if n_req > 2:
        offset = crossed(offset, kv)
    request = ((offset ^ req) << log2(rows_req)) | (req_row & (rows_req - 1))
    kv_request = (((request >> log2(rows_kv)) ^ kv) << log2(rows_kv)) | (request & (rows_kv - 1))
    return (kv_request == kv_row).astype(jnp.bfloat16)


def load_weights_kernel(*refs):
    n = len(refs) // 2
    sem = refs[-1]
    copies = [
        pltpu.make_async_copy(refs[i], refs[n + i], sem.at[i]) for i in range(n)
    ]
    for copy in copies:
        copy.start()
    for copy in copies:
        copy.wait()


def project_kernel(rows_req, n_kv, *refs):
    pieces, (gain, w_query, w_key, w_value, keep, send) = refs[:n_kv], refs[n_kv:]
    rows_kv = pieces[0].shape[0]
    size = rows_kv * n_kv
    order = row_order(size, rows_req, rows_kv, False)
    hidden = jnp.concatenate([piece[...].astype(jnp.float32) for piece in pieces], 0)
    xf = jnp.dot(order, hidden.astype(jnp.bfloat16), preferred_element_type=jnp.float32)
    rows = gain[...].astype(jnp.float32)
    wide_gain = jnp.concatenate([rows[i : i + 1] for i in range(rows.shape[0])], 1)
    scaled = (xf * wide_gain).astype(jnp.bfloat16)
    half = keep.shape[0]

    def put(start, block):
        width = block.shape[1]
        keep[:, start : start + width] = block[:half]
        send[:, start : start + width] = block[half:]

    at = 0
    for weight in (w_query, w_key, w_value):
        put(at, jnp.dot(scaled, weight[...], preferred_element_type=jnp.float32))
        at += weight.shape[1]
    squares = jnp.sum(xf * xf, 1, keepdims=True)
    put(at, jnp.broadcast_to(squares, (size, LANES)))


def plan_of(lengths, sink_count, window):
    count = lengths.shape[0]
    low = jnp.maximum(sink_count, lengths - window)
    first = low // BLOCK
    visits = (lengths - 1) // BLOCK - first + 1
    shift = PLAN_BITS * 2 * jnp.arange(count, dtype=jnp.int32)
    plan = jnp.stack(
        [
            low - first * BLOCK,
            lengths - first * BLOCK,
            jnp.minimum(sink_count, lengths),
            (first | (visits << PLAN_BITS)) << shift,
        ]
    )
    return jnp.broadcast_to(plan[:, :, None], (4, count, LANES))


def visits_of(plan, count):
    mask = (1 << PLAN_BITS) - 1
    packed = sum(plan[3, r : r + 1] for r in range(count))[0, 0]
    fields = [
        lax.shift_right_logical(packed, jnp.int32(PLAN_BITS * i)) & mask for i in range(2 * count)
    ]
    return list(zip(fields[::2], fields[1::2]))


def load_cache_kernel(plan, cache, buf, sem):
    count, blocks = cache.shape[0], cache.shape[2] // BLOCK
    planned = visits_of(plan, count)

    def each(act):
        for r, (first, visits) in enumerate(planned):

            @pl.loop(0, visits)
            def _(t):
                at = (first + t) & (blocks - 1)
                src = pl.ds(pl.multiple_of(at * BLOCK, BLOCK), BLOCK)
                dst = pl.ds(pl.multiple_of(t * BLOCK, BLOCK), BLOCK)
                act(pltpu.make_async_copy(cache.at[r, :, src], buf.at[r, :, dst], sem.at[r, t]))

    each(lambda copy: copy.start())
    each(lambda copy: copy.wait())


def attend_kernel(n_parts, plan, *refs):
    parts = refs[:n_parts]
    (
        cosine,
        sine,
        b_query,
        b_key,
        b_value,
        k_buf,
        v_buf,
        sink_keys,
        sink_values,
        context,
        score_buf,
        q_heads,
        k_extra,
        v_extra,
        result_buf,
    ) = refs[n_parts:]
    count, heads_kv, _, size = k_buf.shape
    q_cols, kv_cols = context.shape[1], heads_kv * size
    group = q_cols // kv_cols
    pad = q_heads.shape[1] // heads_kv
    scale = 1.0 / math.sqrt(size)
    planned = visits_of(plan, count)

    total = parts[0][...]
    for part in parts[1:]:
        total = total + part[...]
    columns = q_cols + 2 * kv_cols
    inv_rms = lax.rsqrt(total[:, columns : columns + 1] / D + EPS)
    bias = jnp.concatenate([b[...].astype(jnp.float32) for b in (b_query, b_key, b_value)], 0)

    def head_of(i):
        return inv_rms * total[:, i * size : (i + 1) * size] + bias[i : i + 1]

    cos, sin = cosine[...], sine[...]

    def rotated(x):
        return x * cos + pltpu.roll(x, size // 2, 1) * sin

    q_heads[...] = jnp.zeros_like(q_heads)
    k_extra[...] = jnp.zeros_like(k_extra)
    v_extra[...] = jnp.zeros_like(v_extra)
    for h in range(heads_kv):
        lanes = slice(h * size, (h + 1) * size)
        for g in range(group):
            head = h * group + g
            block = rotated(head_of(head))
            for r in range(count):
                q_heads[r, h * pad + g : h * pad + g + 1, lanes] = block[r : r + 1]
        k_rot = rotated(head_of(heads_kv * group + h))
        value = head_of(heads_kv * group + heads_kv + h)
        for r in range(count):
            k_extra[r, 0:SINKS, lanes] = sink_keys[r, h].astype(jnp.float32)
            v_extra[r, 0:SINKS, lanes] = sink_values[r, h].astype(jnp.float32)
            k_extra[r, SINKS : SINKS + 1, lanes] = k_rot[r : r + 1]
            v_extra[r, SINKS : SINKS + 1, lanes] = value[r : r + 1]

    contract_last = (((1,), (1,)), ((), ()))
    lane = lax.broadcasted_iota(jnp.int32, (1, EXTRA_ROWS), 1)
    offset = lax.broadcasted_iota(jnp.int32, (1, BLOCK), 1)
    repeats = BLOCK // LANES
    queries = [q_heads[r].astype(jnp.bfloat16) for r in range(count)]

    def both(buf, r, t):
        rows = pl.ds(pl.multiple_of(t * BLOCK, BLOCK), BLOCK)
        return jnp.concatenate([buf[r, h, rows] for h in range(heads_kv)], 1)

    def fold(x, op):
        pieces = [x[:, i : i + LANES] for i in range(0, x.shape[1], LANES)]
        while len(pieces) > 1:
            pieces = [op(*pieces[i : i + 2]) for i in range(0, len(pieces), 2)]
        return pieces[0]

    def score(r, t, last):
        s = (
            lax.dot_general(
                queries[r],
                both(k_buf, r, jnp.minimum(t, last)),
                contract_last,
                preferred_element_type=jnp.float32,
            )
            * scale
        )
        position = t * BLOCK + offset
        low, high = (jnp.concatenate([plan[i, r : r + 1]] * repeats, 1) for i in range(2))
        s = jnp.where((position >= low) & (position < high), s, -jnp.inf)
        score_buf[r, t] = s
        return fold(s, jnp.maximum)

    def mix(r, t, last, top):
        weights = jnp.exp(score_buf[r, t] - top)
        product = jnp.dot(
            weights.astype(jnp.bfloat16),
            both(v_buf, r, jnp.minimum(t, last)),
            preferred_element_type=jnp.float32,
        )
        return fold(weights, jnp.add), product

    def rounds(visits):
        return (visits - 1 + TOGETHER - 1) // TOGETHER

    extras, tops = [], []
    for r in range(count):
        extra = (
            lax.dot_general(
                queries[r],
                k_extra[r].astype(jnp.bfloat16),
                contract_last,
                preferred_element_type=jnp.float32,
            )
            * scale
        )
        live = (lane < plan[2, r : r + 1, :EXTRA_ROWS]) | (lane == SINKS)
        extras.append(jnp.where(live, extra, -jnp.inf))
        tops.append(score(r, 0, 0))
    for r in range(count):
        visits = planned[r][1]

        def more_scores(k, top):
            for i in range(TOGETHER):
                top = jnp.maximum(top, score(r, 1 + k * TOGETHER + i, visits - 1))
            return top

        tops[r] = lax.fori_loop(0, rounds(visits), more_scores, tops[r])
    sums = []
    for r in range(count):
        tops[r] = jnp.maximum(
            jnp.max(tops[r], 1, keepdims=True), jnp.max(extras[r], 1, keepdims=True)
        )
        extras[r] = jnp.exp(extras[r] - tops[r])
        numer = jnp.dot(
            extras[r].astype(jnp.bfloat16),
            v_extra[r].astype(jnp.bfloat16),
            preferred_element_type=jnp.float32,
        )
        denom, product = mix(r, 0, 0, tops[r])
        sums.append((denom, numer + product))
    for r in range(count):
        visits = planned[r][1]

        def more_values(k, carry):
            denom, numer = carry
            for i in range(TOGETHER):
                d, n = mix(r, 1 + k * TOGETHER + i, visits - 1, tops[r])
                denom, numer = denom + d, numer + n
            return denom, numer

        sums[r] = lax.fori_loop(0, rounds(visits), more_values, sums[r])
    for r in range(count):
        denom, numer = sums[r]
        denom = jnp.sum(denom, 1, keepdims=True) + jnp.sum(extras[r], 1, keepdims=True)
        result = numer / denom
        for h in range(heads_kv):
            for g in range(group):
                head = h * group + g
                result_buf[r : r + 1, head * size : (head + 1) * size] = result[
                    h * pad + g : h * pad + g + 1, h * size : (h + 1) * size
                ]
    context[...] = result_buf[...].astype(context.dtype)


def output_kernel(rows_kv, context, w_output, *outs):
    size = context.shape[0]
    rows_req = size // lax.axis_size("req")
    order = row_order(size, rows_req, rows_kv, True)
    rows = jnp.dot(order, context[...], preferred_element_type=jnp.float32).astype(jnp.bfloat16)
    product = jnp.dot(rows, w_output[...], preferred_element_type=jnp.float32)
    for u, out in enumerate(outs):
        out[...] = product[u * rows_kv : (u + 1) * rows_kv]


def spec(space=pltpu.VMEM):
    return pl.BlockSpec(memory_space=space)


def in_hbm(x):
    return pltpu.with_memory_space_constraint(x, pltpu.HBM)


def on_device(
    hidden,
    gain,
    w_query,
    w_key,
    w_value,
    b_query,
    b_key,
    b_value,
    w_output,
    key_cache,
    value_cache,
    sink_keys,
    sink_values,
    lengths,
    sink_count,
    window,
):
    n_req, n_kv = lax.axis_size("req"), lax.axis_size("kv")
    count, heads_kv, cycle, size = key_cache.shape
    rows_kv = hidden.shape[0]
    rows = count * n_req
    q_cols, kv_cols = w_query.shape[1], w_key.shape[1]
    group = q_cols // (heads_kv * size)
    wide = q_cols + 2 * kv_cols + LANES
    f32, bf16 = jnp.float32, jnp.bfloat16

    others = [swap_kv(hidden, n_kv, u) for u in range(1, n_kv)]
    chunk = LANES if gain.shape[0] % LANES == 0 else gain.shape[0]
    wanted = (
        w_query,
        w_key,
        w_value,
        hidden,
        gain.reshape(-1, chunk),
        b_query.reshape(-1, size),
        b_key.reshape(-1, size),
        b_value.reshape(-1, size),
        sink_keys,
        sink_values,
        lengths,
        sink_count,
        window,
    )
    fetched = pl.pallas_call(
        load_weights_kernel,
        out_shape=tuple(jax.ShapeDtypeStruct(w.shape, w.dtype) for w in wanted),
        in_specs=[spec(pltpu.HBM)] * len(wanted),
        out_specs=(spec(),) * len(wanted),
        scratch_shapes=[pltpu.SemaphoreType.DMA((len(wanted),))],
        compiler_params=pltpu.CompilerParams(vmem_limit_bytes=1 << 20),
        cost_estimate=pl.CostEstimate(flops=0, transcendentals=0, bytes_accessed=6 << 20),
        name="load_weights",
    )(*[in_hbm(w) for w in wanted])
    *weights, mine, gain, b_query, b_key, b_value, sink_keys, sink_values = fetched[:-3]
    lengths, sink_count, window = fetched[-3:]
    pieces = [mine] + others
    half = jax.ShapeDtypeStruct((rows // 2, wide), f32)
    keep, send = pl.pallas_call(
        lambda *refs: project_kernel(count, n_kv, *refs),
        out_shape=(half, half),
        in_specs=[spec()] * (n_kv + 4),
        out_specs=(spec(), spec()),
        compiler_params=pltpu.CompilerParams(vmem_limit_bytes=16 << 20),
        name="project",
    )(*pieces, gain, *weights)

    visits = cycle // BLOCK + 1

    def load(cache, plan, name):
        return pl.pallas_call(
            load_cache_kernel,
            out_shape=jax.ShapeDtypeStruct((count, heads_kv, visits * BLOCK, size), bf16),
            in_specs=[spec(), spec(pltpu.HBM)],
            out_specs=spec(),
            scratch_shapes=[pltpu.SemaphoreType.DMA((count, visits))],
            compiler_params=pltpu.CompilerParams(vmem_limit_bytes=1 << 20),
            cost_estimate=pl.CostEstimate(flops=0, transcendentals=0, bytes_accessed=6 << 20),
            name=name,
        )(plan, in_hbm(cache))

    req_stages = stages(n_req, STAGE_BITS)
    plan = plan_of(lengths, sink_count, window)
    keep, plan = lax.optimization_barrier((keep, plan))
    received = swap_req(send, n_req, n_kv, req_stages[0][1])
    k_live = load(key_cache, plan, "load_keys")
    keep, k_live = lax.optimization_barrier((keep, k_live))
    parts = [keep, received]
    for radix, unit in req_stages[1:]:
        x = sum(parts[1:], parts[0])
        chunk = x.shape[0] // radix
        parts = [x[:chunk]] + [
            swap_req(x[q * chunk : (q + 1) * chunk], n_req, n_kv, q * unit)
            for q in range(1, radix)
        ]
    parts[0], plan = lax.optimization_barrier((parts[0], plan))
    v_live = load(value_cache, plan, "load_values")

    freq = jnp.power(1000000.0, -2.0 * jnp.arange(size // 2, dtype=f32) / size)
    angle = lengths.astype(f32)[:, None] * freq
    cos, sin = jnp.cos(angle), jnp.sin(angle)
    cosine = jnp.concatenate([cos, cos], 1)
    sine = jnp.concatenate([-sin, sin], 1)

    pad = -(-group // 8) * 8
    context = pl.pallas_call(
        lambda *refs: attend_kernel(len(parts), *refs),
        out_shape=jax.ShapeDtypeStruct((count, q_cols), bf16),
        in_specs=[spec()] * (len(parts) + 10),
        out_specs=spec(),
        scratch_shapes=[
            pltpu.VMEM((count, visits + TOGETHER, heads_kv * pad, BLOCK), f32),
            pltpu.VMEM((count, heads_kv * pad, heads_kv * size), f32),
            pltpu.VMEM((count, EXTRA_ROWS, heads_kv * size), f32),
            pltpu.VMEM((count, EXTRA_ROWS, heads_kv * size), f32),
            pltpu.VMEM((count, q_cols), f32),
        ],
        compiler_params=pltpu.CompilerParams(vmem_limit_bytes=8 << 20),
        name="attend",
    )(
        plan,
        *parts,
        cosine,
        sine,
        b_query,
        b_key,
        b_value,
        k_live,
        v_live,
        sink_keys,
        sink_values,
    )

    everyone = context
    for radix, unit in reversed(stages(n_req, STAGE_BITS)):
        blocks = [swap_req(everyone, n_req, n_kv, q * unit) for q in range(1, radix)]
        everyone = jnp.concatenate([everyone] + blocks, 0)
    piece = jax.ShapeDtypeStruct((rows_kv, w_output.shape[1]), f32)
    products = pl.pallas_call(
        lambda *refs: output_kernel(rows_kv, *refs),
        out_shape=(piece,) * n_kv,
        in_specs=[spec()] * 2,
        out_specs=(spec(),) * n_kv,
        compiler_params=pltpu.CompilerParams(vmem_limit_bytes=16 << 20),
        name="output",
    )(everyone, w_output)
    result = products[0]
    for u in range(1, n_kv):
        result = result + swap_kv(products[u], n_kv, u)
    return result.astype(bf16)


def solution(mesh):
    in_specs = (
        P("kv", "req"),
        P("req"),
        P("req", "kv"),
        P("req", "kv"),
        P("req", "kv"),
        P("kv"),
        P("kv"),
        P("kv"),
        P("kv", "req"),
        P("req", "kv", None, None),
        P("req", "kv", None, None),
        P("req", "kv", None, None),
        P("req", "kv", None, None),
        P("req"),
        P("req"),
        P("req"),
    )
    out_specs = P("kv", "req")
    return jax.shard_map(
        on_device, mesh=mesh, in_specs=in_specs, out_specs=out_specs, check_vma=False
    )
```

```python
import math

import jax
import jax.numpy as jnp
from jax import lax
from jax.experimental import pallas as pl
from jax.experimental.pallas import tpu as pltpu
from jax.sharding import PartitionSpec as P

D = 5120
SINKS = 4
EPS = 1e-06
BLOCK = 512
PLAN_BITS = 4
TOGETHER = 8
LANES = 128
FAR = 1 << 20
STAGE_BITS = 2

EXTRA_ROWS = 16


def log2(n):
    bits = n.bit_length() - 1
    assert n == 1 << bits
    return bits


def stages(n, most):
    bits = log2(n)
    if bits == 0:
        return []
    result = [(2, 1)]
    left = bits - 1
    while left:
        take = most if left % most == 0 else 1
        left -= take
        result.append((1 << take, 2 << left))
    return result


def crossed(offset, kv):
    low = offset & 3
    turned = ((low & 1) << 1) | (low >> 1)
    return offset ^ ((low ^ turned) * (kv & 1))


def place_to_offset(place, n):
    bits = log2(n)
    if bits == 0:
        return place
    return ((place << 1) | (place >> (bits - 1))) & (n - 1)


def swap_req(x, n_req, n_kv, offset):
    pairs = [
        (i * n_kv + j, (i ^ (crossed(offset, j) if n_req > 2 else offset)) * n_kv + j)
        for i in range(n_req)
        for j in range(n_kv)
    ]
    return lax.ppermute(x, ("req", "kv"), pairs)


def kept(n_kv):
    return [0] + list(range(3, n_kv, 2))


def swap_kv(x, n_kv, offset):
    return lax.ppermute(x, "kv", [(j, j ^ offset) for j in range(n_kv)])


def row_order(size, rows_req, rows_kv, to_kv):
    req, kv = lax.axis_index("req"), lax.axis_index("kv")
    n_req = size // rows_req
    shape = (size, size)
    req_row = lax.broadcasted_iota(jnp.int32, shape, 1 if to_kv else 0)
    kv_row = lax.broadcasted_iota(jnp.int32, shape, 0 if to_kv else 1)
    offset = place_to_offset(req_row >> log2(rows_req), n_req)
    if n_req > 2:
        offset = crossed(offset, kv)
    request = ((offset ^ req) << log2(rows_req)) | (req_row & (rows_req - 1))
    kv_request = (((request >> log2(rows_kv)) ^ kv) << log2(rows_kv)) | (request & (rows_kv - 1))
    return (kv_request == kv_row).astype(jnp.bfloat16)


def load_weights_kernel(*refs):
    n = len(refs) // 2
    sem = refs[-1]
    copies = [
        pltpu.make_async_copy(refs[i], refs[n + i], sem.at[i]) for i in range(n)
    ]
    for copy in copies:
        copy.start()
    for copy in copies:
        copy.wait()


def project_kernel(rows_req, n_kv, *refs):
    pieces, (gain, w_query, w_key, w_value, keep, send) = refs[:n_kv], refs[n_kv:]
    rows_kv = pieces[0].shape[0]
    size = rows_kv * n_kv
    order = row_order(size, rows_req, rows_kv, False)
    hidden = jnp.concatenate([piece[...].astype(jnp.float32) for piece in pieces], 0)
    xf = jnp.dot(order, hidden.astype(jnp.bfloat16), preferred_element_type=jnp.float32)
    rows = gain[...].astype(jnp.float32)
    wide_gain = jnp.concatenate([rows[i : i + 1] for i in range(rows.shape[0])], 1)
    scaled = (xf * wide_gain).astype(jnp.bfloat16)
    half = keep.shape[0]

    def put(start, block):
        width = block.shape[1]
        keep[:, start : start + width] = block[:half]
        send[:, start : start + width] = block[half:]

    at = 0
    for weight in (w_query, w_key, w_value):
        put(at, jnp.dot(scaled, weight[...], preferred_element_type=jnp.float32))
        at += weight.shape[1]
    squares = jnp.sum(xf * xf, 1, keepdims=True)
    put(at, jnp.broadcast_to(squares, (size, LANES)))


def plan_of(lengths, sink_count, window):
    count = lengths.shape[0]
    low = jnp.maximum(sink_count, lengths - window)
    first = low // BLOCK
    visits = (lengths - 1) // BLOCK - first + 1
    shift = PLAN_BITS * 2 * jnp.arange(count, dtype=jnp.int32)
    plan = jnp.stack(
        [
            low - first * BLOCK,
            lengths - first * BLOCK,
            jnp.minimum(sink_count, lengths),
            (first | (visits << PLAN_BITS)) << shift,
        ]
    )
    return jnp.broadcast_to(plan[:, :, None], (4, count, LANES))


def visits_of(plan, count):
    mask = (1 << PLAN_BITS) - 1
    packed = sum(plan[3, r : r + 1] for r in range(count))[0, 0]
    fields = [
        lax.shift_right_logical(packed, jnp.int32(PLAN_BITS * i)) & mask for i in range(2 * count)
    ]
    return list(zip(fields[::2], fields[1::2]))


def load_cache_kernel(plan, cache, buf, sem):
    count, blocks = cache.shape[0], cache.shape[2] // BLOCK
    planned = visits_of(plan, count)

    def each(act):
        for r, (first, visits) in enumerate(planned):

            @pl.loop(0, visits)
            def _(t):
                at = (first + t) & (blocks - 1)
                src = pl.ds(pl.multiple_of(at * BLOCK, BLOCK), BLOCK)
                dst = pl.ds(pl.multiple_of(t * BLOCK, BLOCK), BLOCK)
                act(pltpu.make_async_copy(cache.at[r, :, src], buf.at[r, :, dst], sem.at[r, t]))

    each(lambda copy: copy.start())
    each(lambda copy: copy.wait())


def attend_kernel(n_parts, plan, *refs):
    parts = refs[:n_parts]
    (
        cosine,
        sine,
        b_query,
        b_key,
        b_value,
        k_buf,
        v_buf,
        sink_keys,
        sink_values,
        context,
        score_buf,
        q_heads,
        k_extra,
        v_extra,
        result_buf,
        q_rows,
        tops,
        denoms,
        numers,
    ) = refs[n_parts:]
    count, heads_kv, _, size = k_buf.shape
    q_cols, kv_cols = context.shape[1], heads_kv * size
    group = q_cols // kv_cols
    pad = q_heads.shape[1] // heads_kv
    scale = 1.0 / math.sqrt(size)
    planned = visits_of(plan, count)

    total = parts[0][...]
    for part in parts[1:]:
        total = total + part[...]
    columns = q_cols + 2 * kv_cols
    inv_rms = lax.rsqrt(total[:, columns : columns + 1] / D + EPS)
    bias = jnp.concatenate([b[...].astype(jnp.float32) for b in (b_query, b_key, b_value)], 0)

    def head_of(i):
        return inv_rms * total[:, i * size : (i + 1) * size] + bias[i : i + 1]

    cos, sin = cosine[...], sine[...]

    def rotated(x):
        return x * cos + pltpu.roll(x, size // 2, 1) * sin

    q_heads[...] = jnp.zeros_like(q_heads)
    k_extra[...] = jnp.zeros_like(k_extra)
    v_extra[...] = jnp.zeros_like(v_extra)
    for h in range(heads_kv):
        lanes = slice(h * size, (h + 1) * size)
        for g in range(group):
            head = h * group + g
            block = rotated(head_of(head))
            for r in range(count):
                q_heads[r, h * pad + g : h * pad + g + 1, lanes] = block[r : r + 1]
        k_rot = rotated(head_of(heads_kv * group + h))
        value = head_of(heads_kv * group + heads_kv + h)
        for r in range(count):
            k_extra[r, 0:SINKS, lanes] = sink_keys[r, h].astype(jnp.float32)
            v_extra[r, 0:SINKS, lanes] = sink_values[r, h].astype(jnp.float32)
            k_extra[r, SINKS : SINKS + 1, lanes] = k_rot[r : r + 1]
            v_extra[r, SINKS : SINKS + 1, lanes] = value[r : r + 1]

    contract_last = (((1,), (1,)), ((), ()))
    lane = lax.broadcasted_iota(jnp.int32, (1, EXTRA_ROWS), 1)
    offset = lax.broadcasted_iota(jnp.int32, (1, BLOCK), 1)
    repeats = BLOCK // LANES
    q_rows[...] = q_heads[...].astype(jnp.bfloat16)

    def both(buf, r, t):
        rows = pl.ds(pl.multiple_of(t * BLOCK, BLOCK), BLOCK)
        return jnp.concatenate([buf[r, h, rows] for h in range(heads_kv)], 1)

    def fold(x, op):
        pieces = [x[:, i : i + LANES] for i in range(0, x.shape[1], LANES)]
        while len(pieces) > 1:
            pieces = [op(*pieces[i : i + 2]) for i in range(0, len(pieces), 2)]
        return pieces[0]

    def score(r, t, place, at):
        s = (
            lax.dot_general(
                q_rows[r], both(k_buf, r, t), contract_last, preferred_element_type=jnp.float32
            )
            * scale
        )
        position = at + offset
        low, high = (
            jnp.concatenate([plan[i, pl.ds(r, 1)]] * repeats, 1) for i in range(2)
        )
        s = jnp.where((position >= low) & (position < high), s, -jnp.inf)
        score_buf[place] = s
        return fold(s, jnp.maximum)

    def mix(r, t, place):
        weights = jnp.exp(score_buf[place] - jnp.concatenate([tops[r]] * repeats, 1))
        product = jnp.dot(
            weights.astype(jnp.bfloat16), both(v_buf, r, t), preferred_element_type=jnp.float32
        )
        return fold(weights, jnp.add), product

    starts = [0]
    for _, visits in planned:
        starts.append(starts[-1] + visits - 1)
    left = starts[-1]

    def block_of(place):
        inside = jnp.minimum(place, left - 1)
        r, start = 0, 0
        for i in range(1, count):
            past = inside >= starts[i]
            r = jnp.where(past, i, r)
            start = jnp.where(past, starts[i], start)
        return r, inside - start + 1

    rounds = (left + TOGETHER - 1) // TOGETHER
    extras = []
    for r in range(count):
        extra = (
            lax.dot_general(
                q_rows[r],
                k_extra[r].astype(jnp.bfloat16),
                contract_last,
                preferred_element_type=jnp.float32,
            )
            * scale
        )
        live = (lane < plan[2, r : r + 1, :EXTRA_ROWS]) | (lane == SINKS)
        extras.append(jnp.where(live, extra, -jnp.inf))
        tops[r] = score(r, 0, r, 0)

    @pl.loop(0, rounds)
    def _(k):
        for i in range(TOGETHER):
            place = k * TOGETHER + i
            r, t = block_of(place)
            at = jnp.where(place < left, t * BLOCK, FAR)
            tops[r] = jnp.maximum(tops[r], score(r, t, count + place, at))

    for r in range(count):
        top = jnp.maximum(
            jnp.max(tops[r], 1, keepdims=True), jnp.max(extras[r], 1, keepdims=True)
        )
        tops[r] = jnp.broadcast_to(top, tops.shape[1:])
        extras[r] = jnp.exp(extras[r] - top)
        numer = jnp.dot(
            extras[r].astype(jnp.bfloat16),
            v_extra[r].astype(jnp.bfloat16),
            preferred_element_type=jnp.float32,
        )
        denoms[r], product = mix(r, 0, r)
        numers[r] = numer + product

    @pl.loop(0, rounds)
    def _(k):
        for i in range(TOGETHER):
            place = k * TOGETHER + i
            r, t = block_of(place)
            denom, product = mix(r, t, count + place)
            denoms[r] += denom
            numers[r] += product

    for r in range(count):
        denom = jnp.sum(denoms[r], 1, keepdims=True) + jnp.sum(extras[r], 1, keepdims=True)
        result = numers[r] / denom
        for h in range(heads_kv):
            for g in range(group):
                head = h * group + g
                result_buf[r : r + 1, head * size : (head + 1) * size] = result[
                    h * pad + g : h * pad + g + 1, h * size : (h + 1) * size
                ]
    context[...] = result_buf[...].astype(context.dtype)


def output_kernel(rows_kv, context, w_output, keep, send):
    size = context.shape[0]
    rows_req = size // lax.axis_size("req")
    order = row_order(size, rows_req, rows_kv, True)
    rows = jnp.dot(order, context[...], preferred_element_type=jnp.float32).astype(jnp.bfloat16)
    product = jnp.dot(rows, w_output[...], preferred_element_type=jnp.float32)
    for i, u in enumerate(kept(size // rows_kv)):
        place = slice(i * rows_kv, (i + 1) * rows_kv)
        keep[place] = product[u * rows_kv : (u + 1) * rows_kv]
        send[place] = product[(u ^ 1) * rows_kv : ((u ^ 1) + 1) * rows_kv]


def spec(space=pltpu.VMEM):
    return pl.BlockSpec(memory_space=space)


def attend_call(plan, parts, cosine, sine, b_query, b_key, b_value, k_live, v_live, *sinks):
    count, heads_kv, stored, size = k_live.shape
    group = b_query.shape[0] // heads_kv
    rows, kv_cols = heads_kv * (-(-group // 8) * 8), heads_kv * size
    q_cols = b_query.shape[0] * size
    args = (plan, *parts, cosine, sine, b_query, b_key, b_value, k_live, v_live, *sinks)
    return pl.pallas_call(
        lambda *refs: attend_kernel(len(parts), *refs),
        out_shape=jax.ShapeDtypeStruct((count, q_cols), jnp.bfloat16),
        in_specs=[spec()] * len(args),
        out_specs=spec(),
        scratch_shapes=[
            pltpu.VMEM((count * (stored // BLOCK) + TOGETHER, rows, BLOCK), jnp.float32),
            pltpu.VMEM((count, rows, kv_cols), jnp.float32),
            pltpu.VMEM((count, EXTRA_ROWS, kv_cols), jnp.float32),
            pltpu.VMEM((count, EXTRA_ROWS, kv_cols), jnp.float32),
            pltpu.VMEM((count, q_cols), jnp.float32),
            pltpu.VMEM((count, rows, kv_cols), jnp.bfloat16),
            pltpu.VMEM((count, rows, LANES), jnp.float32),
            pltpu.VMEM((count, rows, LANES), jnp.float32),
            pltpu.VMEM((count, rows, kv_cols), jnp.float32),
        ],
        compiler_params=pltpu.CompilerParams(vmem_limit_bytes=8 << 20),
        name="attend",
    )(*args)


def in_hbm(x):
    return pltpu.with_memory_space_constraint(x, pltpu.HBM)


def on_device(
    hidden,
    gain,
    w_query,
    w_key,
    w_value,
    b_query,
    b_key,
    b_value,
    w_output,
    key_cache,
    value_cache,
    sink_keys,
    sink_values,
    lengths,
    sink_count,
    window,
):
    n_req, n_kv = lax.axis_size("req"), lax.axis_size("kv")
    count, heads_kv, cycle, size = key_cache.shape
    rows_kv = hidden.shape[0]
    rows = count * n_req
    q_cols, kv_cols = w_query.shape[1], w_key.shape[1]
    wide = q_cols + 2 * kv_cols + LANES
    f32, bf16 = jnp.float32, jnp.bfloat16

    others = [swap_kv(hidden, n_kv, u) for u in range(1, n_kv, 2)]
    chunk = LANES if gain.shape[0] % LANES == 0 else gain.shape[0]
    wanted = (
        w_query,
        w_key,
        w_value,
        hidden,
        gain.reshape(-1, chunk),
        b_query.reshape(-1, size),
        b_key.reshape(-1, size),
        b_value.reshape(-1, size),
        sink_keys,
        sink_values,
        lengths,
        sink_count,
        window,
    )
    fetched = pl.pallas_call(
        load_weights_kernel,
        out_shape=tuple(jax.ShapeDtypeStruct(w.shape, w.dtype) for w in wanted),
        in_specs=[spec(pltpu.HBM)] * len(wanted),
        out_specs=(spec(),) * len(wanted),
        scratch_shapes=[pltpu.SemaphoreType.DMA((len(wanted),))],
        compiler_params=pltpu.CompilerParams(vmem_limit_bytes=1 << 20),
        cost_estimate=pl.CostEstimate(flops=0, transcendentals=0, bytes_accessed=6 << 20),
        name="load_weights",
    )(*[in_hbm(w) for w in wanted])
    *weights, mine, gain, b_query, b_key, b_value, sink_keys, sink_values = fetched[:-3]
    lengths, sink_count, window = fetched[-3:]
    pieces = [mine, others[0]]
    for far in others[1:]:
        pieces += [swap_kv(far, n_kv, 1), far]
    half = jax.ShapeDtypeStruct((rows // 2, wide), f32)
    keep, send = pl.pallas_call(
        lambda *refs: project_kernel(count, n_kv, *refs),
        out_shape=(half, half),
        in_specs=[spec()] * (n_kv + 4),
        out_specs=(spec(), spec()),
        compiler_params=pltpu.CompilerParams(vmem_limit_bytes=16 << 20),
        name="project",
    )(*pieces, gain, *weights)

    visits = cycle // BLOCK + 1

    def load(cache, plan, name):
        return pl.pallas_call(
            load_cache_kernel,
            out_shape=jax.ShapeDtypeStruct((count, heads_kv, visits * BLOCK, size), bf16),
            in_specs=[spec(), spec(pltpu.HBM)],
            out_specs=spec(),
            scratch_shapes=[pltpu.SemaphoreType.DMA((count, visits))],
            compiler_params=pltpu.CompilerParams(vmem_limit_bytes=1 << 20),
            cost_estimate=pl.CostEstimate(flops=0, transcendentals=0, bytes_accessed=6 << 20),
            name=name,
        )(plan, in_hbm(cache))

    req_stages = stages(n_req, STAGE_BITS)
    plan = plan_of(lengths, sink_count, window)
    keep, plan = lax.optimization_barrier((keep, plan))
    received = swap_req(send, n_req, n_kv, req_stages[0][1])
    k_live = load(key_cache, plan, "load_keys")
    keep, k_live = lax.optimization_barrier((keep, k_live))
    parts = [keep, received]
    for radix, unit in req_stages[1:]:
        x = sum(parts[1:], parts[0])
        chunk = x.shape[0] // radix
        parts = [x[:chunk]] + [
            swap_req(x[q * chunk : (q + 1) * chunk], n_req, n_kv, q * unit)
            for q in range(1, radix)
        ]
    parts[0], plan = lax.optimization_barrier((parts[0], plan))
    v_live = load(value_cache, plan, "load_values")

    freq = jnp.power(1000000.0, -2.0 * jnp.arange(size // 2, dtype=f32) / size)
    angle = lengths.astype(f32)[:, None] * freq
    cos, sin = jnp.cos(angle), jnp.sin(angle)
    cosine = jnp.concatenate([cos, cos], 1)
    sine = jnp.concatenate([-sin, sin], 1)

    context = attend_call(
        plan, parts, cosine, sine, b_query, b_key, b_value, k_live, v_live, sink_keys, sink_values
    )

    everyone = context
    for radix, unit in reversed(stages(n_req, STAGE_BITS)):
        blocks = [swap_req(everyone, n_req, n_kv, q * unit) for q in range(1, radix)]
        everyone = jnp.concatenate([everyone] + blocks, 0)
    half = jax.ShapeDtypeStruct((rows // 2, w_output.shape[1]), f32)
    keep, send = pl.pallas_call(
        lambda *refs: output_kernel(rows_kv, *refs),
        out_shape=(half, half),
        in_specs=[spec()] * 2,
        out_specs=(spec(), spec()),
        compiler_params=pltpu.CompilerParams(vmem_limit_bytes=16 << 20),
        name="output",
    )(everyone, w_output)
    both = keep + swap_kv(send, n_kv, 1)
    result = both[:rows_kv]
    for i, u in enumerate(kept(n_kv)[1:], 1):
        result = result + swap_kv(both[i * rows_kv : (i + 1) * rows_kv], n_kv, u)
    return result.astype(bf16)


def solution(mesh):
    in_specs = (
        P("kv", "req"),
        P("req"),
        P("req", "kv"),
        P("req", "kv"),
        P("req", "kv"),
        P("kv"),
        P("kv"),
        P("kv"),
        P("kv", "req"),
        P("req", "kv", None, None),
        P("req", "kv", None, None),
        P("req", "kv", None, None),
        P("req", "kv", None, None),
        P("req"),
        P("req"),
        P("req"),
    )
    out_specs = P("kv", "req")
    return jax.shard_map(
        on_device, mesh=mesh, in_specs=in_specs, out_specs=out_specs, check_vma=False
    )
```

```python
import math

import jax
import jax.numpy as jnp
from jax import lax
from jax.experimental import pallas as pl
from jax.experimental.pallas import tpu as pltpu
from jax.sharding import PartitionSpec as P

D = 5120
SINKS = 4
EPS = 1e-06
BLOCK = 512
PLAN_BITS = 4
TOGETHER = 8
LANES = 128
FAR = 1 << 20
EXTRA_ROWS = 16


def log2(n):
    bits = n.bit_length() - 1
    assert n == 1 << bits
    return bits


def stages(n):
    bits = log2(n)
    if bits == 0:
        return []
    result = [(2, 1)]
    left = bits - 1
    while left:
        take = 2 if left % 2 == 0 else 1
        left -= take
        result.append((1 << take, 2 << left))
    return result


def crossed(offset, kv):
    low = offset & 3
    turned = ((low & 1) << 1) | (low >> 1)
    return offset ^ ((low ^ turned) * (kv & 1))


def place_to_offset(place, n, gathered):
    offset = place * 0
    for radix, unit in stages(n) if gathered else reversed(stages(n)):
        offset = offset + (place & (radix - 1)) * unit
        place = place >> log2(radix)
    return offset


def swap_req(x, n_req, n_kv, offset):
    pairs = [
        (i * n_kv + j, (i ^ (crossed(offset, j) if n_req > 2 else offset)) * n_kv + j)
        for i in range(n_req)
        for j in range(n_kv)
    ]
    return lax.ppermute(x, ("req", "kv"), pairs)


def swap_kv(x, n_kv, offset):
    return lax.ppermute(x, "kv", [(j, j ^ offset) for j in range(n_kv)])


def row_order(size, rows_req, rows_kv, to_kv):
    req, kv = lax.axis_index("req"), lax.axis_index("kv")
    n_req = size // rows_req
    shape = (size, size)
    req_row = lax.broadcasted_iota(jnp.int32, shape, 1 if to_kv else 0)
    kv_row = lax.broadcasted_iota(jnp.int32, shape, 0 if to_kv else 1)
    offset = place_to_offset(req_row >> log2(rows_req), n_req, to_kv)
    if n_req > 2:
        offset = crossed(offset, kv)
    request = ((offset ^ req) << log2(rows_req)) | (req_row & (rows_req - 1))
    kv_request = (((request >> log2(rows_kv)) ^ kv) << log2(rows_kv)) | (request & (rows_kv - 1))
    return (kv_request == kv_row).astype(jnp.bfloat16)


def load_weights_kernel(*refs):
    n = len(refs) // 2
    sem = refs[-1]
    copies = [pltpu.make_async_copy(refs[i], refs[n + i], sem.at[i]) for i in range(n)]
    for copy in copies:
        copy.start()
    for copy in copies:
        copy.wait()


def project_kernel(rows_req, n_kv, *refs):
    pieces, (gain, w_query, w_key, w_value, keep, send) = refs[:n_kv], refs[n_kv:]
    rows_kv = pieces[0].shape[0]
    size = rows_kv * n_kv
    order = row_order(size, rows_req, rows_kv, False)
    hidden = jnp.concatenate([piece[...].astype(jnp.float32) for piece in pieces], 0)
    xf = jnp.dot(order, hidden.astype(jnp.bfloat16), preferred_element_type=jnp.float32)
    rows = gain[...].astype(jnp.float32)
    wide_gain = jnp.concatenate([rows[i : i + 1] for i in range(rows.shape[0])], 1)
    scaled = (xf * wide_gain).astype(jnp.bfloat16)
    half = keep.shape[0]

    def put(start, block):
        width = block.shape[1]
        keep[:, start : start + width] = block[:half]
        send[:, start : start + width] = block[half:]

    at = 0
    for weight in (w_query, w_key, w_value):
        put(at, jnp.dot(scaled, weight[...], preferred_element_type=jnp.float32))
        at += weight.shape[1]
    squares = jnp.sum(xf * xf, 1, keepdims=True)
    put(at, jnp.broadcast_to(squares, (size, LANES)))


def plan_of(lengths, sink_count, window):
    count = lengths.shape[0]
    low = jnp.maximum(sink_count, lengths - window)
    first = low // BLOCK
    visits = (lengths - 1) // BLOCK - first + 1
    shift = PLAN_BITS * 2 * jnp.arange(count, dtype=jnp.int32)
    plan = jnp.stack(
        [
            low - first * BLOCK,
            lengths - first * BLOCK,
            jnp.minimum(sink_count, lengths),
            (first | (visits << PLAN_BITS)) << shift,
        ]
    )
    return jnp.broadcast_to(plan[:, :, None], (4, count, LANES))


def visits_of(plan, count):
    mask = (1 << PLAN_BITS) - 1
    packed = sum(plan[3, r : r + 1] for r in range(count))[0, 0]
    fields = [
        lax.shift_right_logical(packed, jnp.int32(PLAN_BITS * i)) & mask for i in range(2 * count)
    ]
    return list(zip(fields[::2], fields[1::2]))


def load_cache_kernel(plan, cache, out, buf, sem):
    count, heads_kv, cycle, size = cache.shape
    planned = visits_of(plan, count)
    target = out if buf is None else buf

    def each(act):
        for r, (first, visits) in enumerate(planned):

            @pl.loop(0, visits)
            def _(t):
                at = (first + t) & (cycle // BLOCK - 1)
                src = pl.ds(pl.multiple_of(at * BLOCK, BLOCK), BLOCK)
                dst = pl.ds(pl.multiple_of(t * BLOCK, BLOCK), BLOCK)
                copy = pltpu.make_async_copy(
                    cache.at[r, :, src], target.at[r, :, dst], sem.at[r, t]
                )
                act(copy, r, dst)

    def finish(copy, r, slots):
        copy.wait()
        if buf is not None:
            for h in range(heads_kv):
                out[r, h * size : (h + 1) * size, slots] = buf[r, h, slots].T

    each(lambda copy, r, slots: copy.start())
    each(finish)


def attend_kernel(n_parts, plan, *refs):
    parts = refs[:n_parts]
    (
        cosine,
        sine,
        b_query,
        b_key,
        b_value,
        k_buf,
        v_buf,
        sink_keys,
        sink_values,
        context,
        score_buf,
        q_heads,
        k_extra,
        v_extra,
        result_buf,
        q_rows,
        tops,
        denoms,
        numers,
    ) = refs[n_parts:]
    count, heads_kv, _, size = v_buf.shape
    q_cols, kv_cols = context.shape[1], heads_kv * size
    group = q_cols // kv_cols
    pad = q_heads.shape[1] // heads_kv
    scale = 1.0 / math.sqrt(size)
    planned = visits_of(plan, count)

    total = parts[0][...]
    for part in parts[1:]:
        total = total + part[...]
    columns = q_cols + 2 * kv_cols
    inv_rms = lax.rsqrt(total[:, columns : columns + 1] / D + EPS)
    bias = jnp.concatenate([b[...].astype(jnp.float32) for b in (b_query, b_key, b_value)], 0)

    def head_of(i):
        return inv_rms * total[:, i * size : (i + 1) * size] + bias[i : i + 1]

    cos, sin = cosine[...], sine[...]

    def rotated(x):
        return x * cos + pltpu.roll(x, size // 2, 1) * sin

    q_heads[...] = jnp.zeros_like(q_heads)
    k_extra[...] = jnp.zeros_like(k_extra)
    v_extra[...] = jnp.zeros_like(v_extra)
    for h in range(heads_kv):
        lanes = slice(h * size, (h + 1) * size)
        for g in range(group):
            head = h * group + g
            block = rotated(head_of(head))
            for r in range(count):
                q_heads[r, h * pad + g : h * pad + g + 1, lanes] = block[r : r + 1]
        k_rot = rotated(head_of(heads_kv * group + h))
        value = head_of(heads_kv * group + heads_kv + h)
        for r in range(count):
            k_extra[r, 0:SINKS, lanes] = sink_keys[r, h].astype(jnp.float32)
            v_extra[r, 0:SINKS, lanes] = sink_values[r, h].astype(jnp.float32)
            k_extra[r, SINKS : SINKS + 1, lanes] = k_rot[r : r + 1]
            v_extra[r, SINKS : SINKS + 1, lanes] = value[r : r + 1]

    contract_last = (((1,), (1,)), ((), ()))
    lane = lax.broadcasted_iota(jnp.int32, (1, EXTRA_ROWS), 1)
    offset = lax.broadcasted_iota(jnp.int32, (1, BLOCK), 1)
    repeats = BLOCK // LANES
    q_rows[...] = q_heads[...].astype(jnp.bfloat16)

    def both(buf, r, t):
        rows = pl.ds(pl.multiple_of(t * BLOCK, BLOCK), BLOCK)
        return jnp.concatenate([buf[r, h, rows] for h in range(heads_kv)], 1)

    def fold(x, op):
        pieces = [x[:, i : i + LANES] for i in range(0, x.shape[1], LANES)]
        while len(pieces) > 1:
            pieces = [op(*pieces[i : i + 2]) for i in range(0, len(pieces), 2)]
        return pieces[0]

    def score(r, t, place, at):
        s = (
            jnp.dot(
                q_rows[r],
                k_buf[r, :, pl.ds(pl.multiple_of(t * BLOCK, BLOCK), BLOCK)],
                preferred_element_type=jnp.float32,
            )
            * scale
        )
        position = at + offset
        low, high = (
            jnp.concatenate([plan[i, pl.ds(r, 1)]] * repeats, 1) for i in range(2)
        )
        s = jnp.where((position >= low) & (position < high), s, -jnp.inf)
        score_buf[place] = s
        return fold(s, jnp.maximum)

    def mix(r, t, place):
        weights = jnp.exp(score_buf[place] - jnp.concatenate([tops[r]] * repeats, 1))
        product = jnp.dot(
            weights.astype(jnp.bfloat16), both(v_buf, r, t), preferred_element_type=jnp.float32
        )
        return fold(weights, jnp.add), product

    starts = [0]
    for _, visits in planned:
        starts.append(starts[-1] + visits - 1)
    left = starts[-1]

    def block_of(place):
        inside = jnp.minimum(place, left - 1)
        r, start = 0, 0
        for i in range(1, count):
            past = inside >= starts[i]
            r = jnp.where(past, i, r)
            start = jnp.where(past, starts[i], start)
        return r, inside - start + 1

    tail = TOGETHER // 2
    spare = left & (TOGETHER - 1)
    rounds = (left >> log2(TOGETHER)) + jnp.where(spare > tail, 1, 0)
    tails = jnp.where((spare > 0) & (spare <= tail), 1, 0)
    extras = []
    for r in range(count):
        extra = (
            lax.dot_general(
                q_rows[r],
                k_extra[r].astype(jnp.bfloat16),
                contract_last,
                preferred_element_type=jnp.float32,
            )
            * scale
        )
        live = (lane < plan[2, r : r + 1, :EXTRA_ROWS]) | (lane == SINKS)
        extras.append(jnp.where(live, extra, -jnp.inf))
        tops[r] = score(r, 0, r, 0)

    def score_some(start, number):
        for i in range(number):
            place = start + i
            r, t = block_of(place)
            at = jnp.where(place < left, t * BLOCK, FAR)
            tops[r] = jnp.maximum(tops[r], score(r, t, count + place, at))

    def mix_some(start, number):
        for i in range(number):
            place = start + i
            r, t = block_of(place)
            denom, product = mix(r, t, count + place)
            denoms[r] += denom
            numers[r] += product

    def all_others(some):
        pl.loop(0, rounds)(lambda k: some(k * TOGETHER, TOGETHER))
        pl.loop(0, tails)(lambda k: some(rounds * TOGETHER, tail))

    all_others(score_some)
    for r in range(count):
        top = jnp.maximum(
            jnp.max(tops[r], 1, keepdims=True), jnp.max(extras[r], 1, keepdims=True)
        )
        tops[r] = jnp.broadcast_to(top, tops.shape[1:])
        extras[r] = jnp.exp(extras[r] - top)
        numer = jnp.dot(
            extras[r].astype(jnp.bfloat16),
            v_extra[r].astype(jnp.bfloat16),
            preferred_element_type=jnp.float32,
        )
        denoms[r], product = mix(r, 0, r)
        numers[r] = numer + product

    all_others(mix_some)

    for r in range(count):
        denom = jnp.sum(denoms[r], 1, keepdims=True) + jnp.sum(extras[r], 1, keepdims=True)
        result = numers[r] / denom
        for h in range(heads_kv):
            for g in range(group):
                head = h * group + g
                result_buf[r : r + 1, head * size : (head + 1) * size] = result[
                    h * pad + g : h * pad + g + 1, h * size : (h + 1) * size
                ]
    context[...] = result_buf[...].astype(context.dtype)


def output_kernel(context, w_output, *outs):
    size, rows_kv = context.shape[0], outs[0].shape[0]
    rows_req = size // lax.axis_size("req")
    order = row_order(size, rows_req, rows_kv, True)
    rows = jnp.dot(order, context[...], preferred_element_type=jnp.float32).astype(jnp.bfloat16)
    product = jnp.dot(rows, w_output[...], preferred_element_type=jnp.float32)
    for i, out in enumerate(outs):
        out[...] = product[i * rows_kv : (i + 1) * rows_kv]


def spec(space=pltpu.VMEM):
    return pl.BlockSpec(memory_space=space)


def attend_call(plan, parts, cosine, sine, b_query, b_key, b_value, k_live, v_live, *sinks):
    count, heads_kv, stored, size = v_live.shape
    group = b_query.shape[0] // heads_kv
    rows, kv_cols = heads_kv * (-(-group // 8) * 8), heads_kv * size
    q_cols = b_query.shape[0] * size
    args = (plan, *parts, cosine, sine, b_query, b_key, b_value, k_live, v_live, *sinks)
    return pl.pallas_call(
        lambda *refs: attend_kernel(len(parts), *refs),
        out_shape=jax.ShapeDtypeStruct((count, q_cols), jnp.bfloat16),
        in_specs=[spec()] * len(args),
        out_specs=spec(),
        scratch_shapes=[
            pltpu.VMEM((count * (stored // BLOCK) + TOGETHER, rows, BLOCK), jnp.float32),
            pltpu.VMEM((count, rows, kv_cols), jnp.float32),
            pltpu.VMEM((count, EXTRA_ROWS, kv_cols), jnp.float32),
            pltpu.VMEM((count, EXTRA_ROWS, kv_cols), jnp.float32),
            pltpu.VMEM((count, q_cols), jnp.float32),
            pltpu.VMEM((count, rows, kv_cols), jnp.bfloat16),
            pltpu.VMEM((count, rows, LANES), jnp.float32),
            pltpu.VMEM((count, rows, LANES), jnp.float32),
            pltpu.VMEM((count, rows, kv_cols), jnp.float32),
        ],
        compiler_params=pltpu.CompilerParams(vmem_limit_bytes=8 << 20),
        name="attend",
    )(*args)


def in_hbm(x):
    return pltpu.with_memory_space_constraint(x, pltpu.HBM)


def on_device(
    hidden,
    gain,
    w_query,
    w_key,
    w_value,
    b_query,
    b_key,
    b_value,
    w_output,
    key_cache,
    value_cache,
    sink_keys,
    sink_values,
    lengths,
    sink_count,
    window,
):
    n_req, n_kv = lax.axis_size("req"), lax.axis_size("kv")
    count, heads_kv, cycle, size = key_cache.shape
    rows_kv = hidden.shape[0]
    rows = count * n_req
    q_cols, kv_cols = w_query.shape[1], w_key.shape[1]
    wide = q_cols + 2 * kv_cols + LANES
    f32, bf16 = jnp.float32, jnp.bfloat16

    others = [swap_kv(hidden, n_kv, u) for u in range(1, n_kv, 2)]
    chunk = LANES if gain.shape[0] % LANES == 0 else gain.shape[0]
    wanted = (
        w_query,
        w_key,
        w_value,
        hidden,
        gain.reshape(-1, chunk),
        b_query.reshape(-1, size),
        b_key.reshape(-1, size),
        b_value.reshape(-1, size),
        sink_keys,
        sink_values,
        lengths,
        sink_count,
        window,
    )
    fetched = pl.pallas_call(
        load_weights_kernel,
        out_shape=tuple(jax.ShapeDtypeStruct(w.shape, w.dtype) for w in wanted),
        in_specs=[spec(pltpu.HBM)] * len(wanted),
        out_specs=(spec(),) * len(wanted),
        scratch_shapes=[pltpu.SemaphoreType.DMA((len(wanted),))],
        compiler_params=pltpu.CompilerParams(vmem_limit_bytes=1 << 20),
        cost_estimate=pl.CostEstimate(flops=0, transcendentals=0, bytes_accessed=6 << 20),
        name="load_weights",
    )(*[in_hbm(w) for w in wanted])
    *weights, mine, gain, b_query, b_key, b_value, sink_keys, sink_values = fetched[:-3]
    lengths, sink_count, window = fetched[-3:]
    pieces = [mine, others[0]]
    for far in others[1:]:
        pieces += [swap_kv(far, n_kv, 1), far]
    half = jax.ShapeDtypeStruct((rows // 2, wide), f32)
    keep, send = pl.pallas_call(
        lambda *refs: project_kernel(count, n_kv, *refs),
        out_shape=(half, half),
        in_specs=[spec()] * (n_kv + 4),
        out_specs=(spec(), spec()),
        compiler_params=pltpu.CompilerParams(vmem_limit_bytes=16 << 20),
        name="project",
    )(*pieces, gain, *weights)

    visits = cycle // BLOCK + 1

    def load(cache, plan, turn, name):
        loaded = (count, heads_kv, visits * BLOCK, size)
        turned = (count, heads_kv * size, visits * BLOCK)
        sem = pltpu.SemaphoreType.DMA((count, visits))
        kernel = load_cache_kernel
        if not turn:
            kernel = lambda plan, cache, out, sem: load_cache_kernel(plan, cache, out, None, sem)
        return pl.pallas_call(
            kernel,
            out_shape=jax.ShapeDtypeStruct(turned if turn else loaded, bf16),
            in_specs=[spec(), spec(pltpu.HBM)],
            out_specs=spec(),
            scratch_shapes=([pltpu.VMEM(loaded, bf16)] if turn else []) + [sem],
            compiler_params=pltpu.CompilerParams(vmem_limit_bytes=(12 if turn else 1) << 20),
            cost_estimate=pl.CostEstimate(flops=0, transcendentals=0, bytes_accessed=6 << 20),
            name=name,
        )(plan, in_hbm(cache))

    req_stages = stages(n_req)
    plan = plan_of(lengths, sink_count, window)
    keep, plan = lax.optimization_barrier((keep, plan))
    received = swap_req(send, n_req, n_kv, req_stages[0][1])
    k_live = load(key_cache, plan, True, "load_keys")
    keep, k_live = lax.optimization_barrier((keep, k_live))
    parts = [keep, received]
    for radix, unit in req_stages[1:]:
        x = sum(parts[1:], parts[0])
        chunk = x.shape[0] // radix
        parts = [x[:chunk]] + [
            swap_req(x[q * chunk : (q + 1) * chunk], n_req, n_kv, q * unit)
            for q in range(1, radix)
        ]
    parts[0], plan = lax.optimization_barrier((parts[0], plan))
    v_live = load(value_cache, plan, False, "load_values")

    freq = jnp.power(1000000.0, -2.0 * jnp.arange(size // 2, dtype=f32) / size)
    angle = lengths.astype(f32)[:, None] * freq
    cos, sin = jnp.cos(angle), jnp.sin(angle)
    cosine = jnp.concatenate([cos, cos], 1)
    sine = jnp.concatenate([-sin, sin], 1)

    context = attend_call(
        plan, parts, cosine, sine, b_query, b_key, b_value, k_live, v_live, sink_keys, sink_values
    )

    everyone = context
    for radix, unit in stages(n_req):
        blocks = [swap_req(everyone, n_req, n_kv, q * unit) for q in range(1, radix)]
        everyone = jnp.concatenate([everyone] + blocks, 0)
    piece = jax.ShapeDtypeStruct((rows_kv, w_output.shape[1]), f32)
    products = pl.pallas_call(
        output_kernel,
        out_shape=(piece,) * n_kv,
        in_specs=[spec()] * 2,
        out_specs=(spec(),) * n_kv,
        compiler_params=pltpu.CompilerParams(vmem_limit_bytes=16 << 20),
        name="output",
    )(everyone, w_output)
    result = products[0]
    for u in range(n_kv - 1, 0, -1):
        result = result + swap_kv(products[u], n_kv, u)
    return result.astype(bf16)


def solution(mesh):
    in_specs = (
        P("kv", "req"),
        P("req"),
        P("req", "kv"),
        P("req", "kv"),
        P("req", "kv"),
        P("kv"),
        P("kv"),
        P("kv"),
        P("kv", "req"),
        P("req", "kv", None, None),
        P("req", "kv", None, None),
        P("req", "kv", None, None),
        P("req", "kv", None, None),
        P("req"),
        P("req"),
        P("req"),
    )
    out_specs = P("kv", "req")
    return jax.shard_map(
        on_device, mesh=mesh, in_specs=in_specs, out_specs=out_specs, check_vma=False
    )
```

```python
import functools
import math

import jax
import jax.numpy as jnp
from jax import lax
from jax.experimental import pallas as pl
from jax.experimental.pallas import tpu as pltpu
from jax.sharding import PartitionSpec as P

D = 5120
SINKS = 4
EPS = 1e-06
BLOCK = 512
PLAN_BITS = 4
TOGETHER = 16
STEP = 2
LANES = 128
FAR = 1 << 20
EXTRA_ROWS = 16


def log2(n):
    bits = n.bit_length() - 1
    assert n == 1 << bits
    return bits


def stages(n):
    bits = log2(n)
    if bits == 0:
        return []
    result = [(2, 1)]
    left = bits - 1
    while left:
        take = 2 if left % 2 == 0 else 1
        left -= take
        result.append((1 << take, 2 << left))
    return result


def crossed(offset, kv):
    low = offset & 3
    turned = ((low & 1) << 1) | (low >> 1)
    return offset ^ ((low ^ turned) * (kv & 1))


def place_to_offset(place, n, gathered):
    offset = place * 0
    for radix, unit in stages(n) if gathered else reversed(stages(n)):
        offset = offset + (place & (radix - 1)) * unit
        place = place >> log2(radix)
    return offset


def swap_req(x, n_req, n_kv, offset):
    pairs = [
        (i * n_kv + j, (i ^ (crossed(offset, j) if n_req > 2 else offset)) * n_kv + j)
        for i in range(n_req)
        for j in range(n_kv)
    ]
    return lax.ppermute(x, ("req", "kv"), pairs)


def swap_kv(x, n_kv, offset):
    return lax.ppermute(x, "kv", [(j, j ^ offset) for j in range(n_kv)])


def row_order(size, rows_req, rows_kv, to_kv):
    req, kv = lax.axis_index("req"), lax.axis_index("kv")
    n_req = size // rows_req
    shape = (size, size)
    req_row = lax.broadcasted_iota(jnp.int32, shape, 1 if to_kv else 0)
    kv_row = lax.broadcasted_iota(jnp.int32, shape, 0 if to_kv else 1)
    offset = place_to_offset(req_row >> log2(rows_req), n_req, to_kv)
    if n_req > 2:
        offset = crossed(offset, kv)
    request = ((offset ^ req) << log2(rows_req)) | (req_row & (rows_req - 1))
    kv_request = (((request >> log2(rows_kv)) ^ kv) << log2(rows_kv)) | (request & (rows_kv - 1))
    return (kv_request == kv_row).astype(jnp.bfloat16)


def load_weights_kernel(*refs):
    n = len(refs) // 2
    sem = refs[-1]
    copies = [pltpu.make_async_copy(refs[i], refs[n + i], sem.at[i]) for i in range(n)]
    for copy in copies:
        copy.start()
    for copy in copies:
        copy.wait()


def project_kernel(rows_req, n_kv, *refs):
    pieces, (gain, w_query, w_key, w_value, keep, send) = refs[:n_kv], refs[n_kv:]
    rows_kv = pieces[0].shape[0]
    size = rows_kv * n_kv
    order = row_order(size, rows_req, rows_kv, False)
    hidden = jnp.concatenate([piece[...].astype(jnp.float32) for piece in pieces], 0)
    xf = jnp.dot(order, hidden.astype(jnp.bfloat16), preferred_element_type=jnp.float32)
    rows = gain[...].astype(jnp.float32)
    wide_gain = jnp.concatenate([rows[i : i + 1] for i in range(rows.shape[0])], 1)
    scaled = (xf * wide_gain).astype(jnp.bfloat16)
    half = keep.shape[0]

    def put(start, block):
        width = block.shape[1]
        keep[:, start : start + width] = block[:half]
        send[:, start : start + width] = block[half:]

    at = 0
    for weight in (w_query, w_key, w_value):
        put(at, jnp.dot(scaled, weight[...], preferred_element_type=jnp.float32))
        at += weight.shape[1]
    squares = jnp.sum(xf * xf, 1, keepdims=True)
    put(at, jnp.broadcast_to(squares, (size, LANES)))


def plan_of(lengths, sink_count, window):
    count = lengths.shape[0]
    low = jnp.maximum(sink_count, lengths - window)
    first = low // BLOCK
    visits = (lengths - 1) // BLOCK - first + 1
    shift = PLAN_BITS * 2 * jnp.arange(count, dtype=jnp.int32)
    plan = jnp.stack(
        [
            low - first * BLOCK,
            lengths - first * BLOCK,
            jnp.minimum(sink_count, lengths),
            (first | (visits << PLAN_BITS)) << shift,
        ]
    )
    return jnp.broadcast_to(plan[:, :, None], (4, count, LANES))


def visits_of(plan, count):
    mask = (1 << PLAN_BITS) - 1
    packed = sum(plan[3, r : r + 1] for r in range(count))[0, 0]
    fields = [
        lax.shift_right_logical(packed, jnp.int32(PLAN_BITS * i)) & mask for i in range(2 * count)
    ]
    return list(zip(fields[::2], fields[1::2]))


def load_cache_kernel(plan, cache, out, buf, sem):
    count, heads_kv, cycle, size = cache.shape
    planned = visits_of(plan, count)
    target = out if buf is None else buf

    def each(act):
        for r, (first, visits) in enumerate(planned):

            @pl.loop(0, visits)
            def _(t):
                at = (first + t) & (cycle // BLOCK - 1)
                src = pl.ds(pl.multiple_of(at * BLOCK, BLOCK), BLOCK)
                dst = pl.ds(pl.multiple_of(t * BLOCK, BLOCK), BLOCK)
                copy = pltpu.make_async_copy(
                    cache.at[r, :, src], target.at[r, :, dst], sem.at[r, t]
                )
                act(copy, r, dst)

    def finish(copy, r, slots):
        copy.wait()
        if buf is not None:
            for h in range(heads_kv):
                out[r, h * size : (h + 1) * size, slots] = buf[r, h, slots].T

    each(lambda copy, r, slots: copy.start())
    each(finish)


def attend_kernel(n_parts, plan, *refs):
    parts = refs[:n_parts]
    (
        cosine,
        sine,
        b_query,
        b_key,
        b_value,
        k_buf,
        v_buf,
        sink_keys,
        sink_values,
        context,
        score_buf,
        q_heads,
        k_extra,
        v_extra,
        result_buf,
        q_rows,
        tops,
        denoms,
        numers,
    ) = refs[n_parts:]
    count, heads_kv, _, size = v_buf.shape
    q_cols, kv_cols = context.shape[1], heads_kv * size
    group = q_cols // kv_cols
    pad = q_heads.shape[1] // heads_kv
    scale = 1.0 / math.sqrt(size)
    planned = visits_of(plan, count)

    total = parts[0][...]
    for part in parts[1:]:
        total = total + part[...]
    columns = q_cols + 2 * kv_cols
    inv_rms = lax.rsqrt(total[:, columns : columns + 1] / D + EPS)
    bias = jnp.concatenate([b[...].astype(jnp.float32) for b in (b_query, b_key, b_value)], 0)

    def head_of(i):
        return inv_rms * total[:, i * size : (i + 1) * size] + bias[i : i + 1]

    cos, sin = cosine[...], sine[...]

    def rotated(x):
        return x * cos + pltpu.roll(x, size // 2, 1) * sin

    q_heads[...] = jnp.zeros_like(q_heads)
    k_extra[...] = jnp.zeros_like(k_extra)
    v_extra[...] = jnp.zeros_like(v_extra)
    for h in range(heads_kv):
        lanes = slice(h * size, (h + 1) * size)
        for g in range(group):
            head = h * group + g
            block = rotated(head_of(head))
            for r in range(count):
                q_heads[r, h * pad + g : h * pad + g + 1, lanes] = block[r : r + 1]
        k_rot = rotated(head_of(heads_kv * group + h))
        value = head_of(heads_kv * group + heads_kv + h)
        for r in range(count):
            k_extra[r, 0:SINKS, lanes] = sink_keys[r, h].astype(jnp.float32)
            v_extra[r, 0:SINKS, lanes] = sink_values[r, h].astype(jnp.float32)
            k_extra[r, SINKS : SINKS + 1, lanes] = k_rot[r : r + 1]
            v_extra[r, SINKS : SINKS + 1, lanes] = value[r : r + 1]

    contract_last = (((1,), (1,)), ((), ()))
    lane = lax.broadcasted_iota(jnp.int32, (1, EXTRA_ROWS), 1)
    offset = lax.broadcasted_iota(jnp.int32, (1, BLOCK), 1)
    repeats = BLOCK // LANES
    q_rows[...] = q_heads[...].astype(jnp.bfloat16)

    def both(buf, r, t):
        rows = pl.ds(pl.multiple_of(t * BLOCK, BLOCK), BLOCK)
        return jnp.concatenate([buf[r, h, rows] for h in range(heads_kv)], 1)

    def fold(x, op):
        pieces = [x[:, i : i + LANES] for i in range(0, x.shape[1], LANES)]
        while len(pieces) > 1:
            pieces = [op(*pieces[i : i + 2]) for i in range(0, len(pieces), 2)]
        return pieces[0]

    def score(r, t, place, at):
        s = (
            jnp.dot(
                q_rows[r],
                k_buf[r, :, pl.ds(pl.multiple_of(t * BLOCK, BLOCK), BLOCK)],
                preferred_element_type=jnp.float32,
            )
            * scale
        )
        position = at + offset
        low, high = (
            jnp.concatenate([plan[i, pl.ds(r, 1)]] * repeats, 1) for i in range(2)
        )
        s = jnp.where((position >= low) & (position < high), s, -jnp.inf)
        score_buf[place] = s
        return fold(s, jnp.maximum)

    def mix(r, t, place):
        weights = jnp.exp(score_buf[place] - jnp.concatenate([tops[r]] * repeats, 1))
        product = jnp.dot(
            weights.astype(jnp.bfloat16), both(v_buf, r, t), preferred_element_type=jnp.float32
        )
        return fold(weights, jnp.add), product

    starts = [0]
    for _, visits in planned:
        starts.append(starts[-1] + visits - 1)
    left = starts[-1]

    def block_of(place):
        inside = jnp.minimum(place, left - 1)
        r, start = 0, 0
        for i in range(1, count):
            past = inside >= starts[i]
            r = jnp.where(past, i, r)
            start = jnp.where(past, starts[i], start)
        return r, inside - start + 1

    rounds = left >> log2(TOGETHER)
    rest = left & (TOGETHER - 1)
    extras = []
    for r in range(count):
        extra = (
            lax.dot_general(
                q_rows[r],
                k_extra[r].astype(jnp.bfloat16),
                contract_last,
                preferred_element_type=jnp.float32,
            )
            * scale
        )
        live = (lane < plan[2, r : r + 1, :EXTRA_ROWS]) | (lane == SINKS)
        extras.append(jnp.where(live, extra, -jnp.inf))
        tops[r] = score(r, 0, r, 0)

    def score_some(start, number):
        for i in range(number):
            place = start + i
            r, t = block_of(place)
            at = jnp.where(place < left, t * BLOCK, FAR)
            tops[r] = jnp.maximum(tops[r], score(r, t, count + place, at))

    def mix_some(start, number):
        for i in range(number):
            place = start + i
            r, t = block_of(place)
            denom, product = mix(r, t, count + place)
            denoms[r] += denom
            numers[r] += product

    def all_others(some):
        pl.loop(0, rounds)(lambda k: some(k * TOGETHER, TOGETHER))
        for size in range(STEP, TOGETHER + 1, STEP):
            fits = (rest > size - STEP) & (rest <= size)
            pl.when(fits)(functools.partial(some, rounds * TOGETHER, size))

    all_others(score_some)
    for r in range(count):
        top = jnp.maximum(
            jnp.max(tops[r], 1, keepdims=True), jnp.max(extras[r], 1, keepdims=True)
        )
        tops[r] = jnp.broadcast_to(top, tops.shape[1:])
        extras[r] = jnp.exp(extras[r] - top)
        numer = jnp.dot(
            extras[r].astype(jnp.bfloat16),
            v_extra[r].astype(jnp.bfloat16),
            preferred_element_type=jnp.float32,
        )
        denoms[r], product = mix(r, 0, r)
        numers[r] = numer + product

    all_others(mix_some)

    for r in range(count):
        denom = jnp.sum(denoms[r], 1, keepdims=True) + jnp.sum(extras[r], 1, keepdims=True)
        result = numers[r] / denom
        for h in range(heads_kv):
            for g in range(group):
                head = h * group + g
                result_buf[r : r + 1, head * size : (head + 1) * size] = result[
                    h * pad + g : h * pad + g + 1, h * size : (h + 1) * size
                ]
    context[...] = result_buf[...].astype(context.dtype)


def output_kernel(context, w_output, *outs):
    size, rows_kv = context.shape[0], outs[0].shape[0]
    rows_req = size // lax.axis_size("req")
    order = row_order(size, rows_req, rows_kv, True)
    rows = jnp.dot(order, context[...], preferred_element_type=jnp.float32).astype(jnp.bfloat16)
    product = jnp.dot(rows, w_output[...], preferred_element_type=jnp.float32)
    for i, out in enumerate(outs):
        out[...] = product[i * rows_kv : (i + 1) * rows_kv]


def spec(space=pltpu.VMEM):
    return pl.BlockSpec(memory_space=space)


def attend_call(plan, parts, cosine, sine, b_query, b_key, b_value, k_live, v_live, *sinks):
    count, heads_kv, stored, size = v_live.shape
    group = b_query.shape[0] // heads_kv
    rows, kv_cols = heads_kv * (-(-group // 8) * 8), heads_kv * size
    q_cols = b_query.shape[0] * size
    args = (plan, *parts, cosine, sine, b_query, b_key, b_value, k_live, v_live, *sinks)
    return pl.pallas_call(
        lambda *refs: attend_kernel(len(parts), *refs),
        out_shape=jax.ShapeDtypeStruct((count, q_cols), jnp.bfloat16),
        in_specs=[spec()] * len(args),
        out_specs=spec(),
        scratch_shapes=[
            pltpu.VMEM((count * (stored // BLOCK) + TOGETHER, rows, BLOCK), jnp.float32),
            pltpu.VMEM((count, rows, kv_cols), jnp.float32),
            pltpu.VMEM((count, EXTRA_ROWS, kv_cols), jnp.float32),
            pltpu.VMEM((count, EXTRA_ROWS, kv_cols), jnp.float32),
            pltpu.VMEM((count, q_cols), jnp.float32),
            pltpu.VMEM((count, rows, kv_cols), jnp.bfloat16),
            pltpu.VMEM((count, rows, LANES), jnp.float32),
            pltpu.VMEM((count, rows, LANES), jnp.float32),
            pltpu.VMEM((count, rows, kv_cols), jnp.float32),
        ],
        compiler_params=pltpu.CompilerParams(vmem_limit_bytes=8 << 20),
        name="attend",
    )(*args)


def in_hbm(x):
    return pltpu.with_memory_space_constraint(x, pltpu.HBM)


def on_device(
    hidden,
    gain,
    w_query,
    w_key,
    w_value,
    b_query,
    b_key,
    b_value,
    w_output,
    key_cache,
    value_cache,
    sink_keys,
    sink_values,
    lengths,
    sink_count,
    window,
):
    n_req, n_kv = lax.axis_size("req"), lax.axis_size("kv")
    count, heads_kv, cycle, size = key_cache.shape
    rows_kv = hidden.shape[0]
    rows = count * n_req
    q_cols, kv_cols = w_query.shape[1], w_key.shape[1]
    wide = q_cols + 2 * kv_cols + LANES
    f32, bf16 = jnp.float32, jnp.bfloat16

    others = [swap_kv(hidden, n_kv, u) for u in range(1, n_kv, 2)]
    chunk = LANES if gain.shape[0] % LANES == 0 else gain.shape[0]
    wanted = (
        w_query,
        w_key,
        w_value,
        hidden,
        gain.reshape(-1, chunk),
        b_query.reshape(-1, size),
        b_key.reshape(-1, size),
        b_value.reshape(-1, size),
        sink_keys,
        sink_values,
        lengths,
        sink_count,
        window,
    )
    fetched = pl.pallas_call(
        load_weights_kernel,
        out_shape=tuple(jax.ShapeDtypeStruct(w.shape, w.dtype) for w in wanted),
        in_specs=[spec(pltpu.HBM)] * len(wanted),
        out_specs=(spec(),) * len(wanted),
        scratch_shapes=[pltpu.SemaphoreType.DMA((len(wanted),))],
        compiler_params=pltpu.CompilerParams(vmem_limit_bytes=1 << 20),
        cost_estimate=pl.CostEstimate(flops=0, transcendentals=0, bytes_accessed=6 << 20),
        name="load_weights",
    )(*[in_hbm(w) for w in wanted])
    *weights, mine, gain, b_query, b_key, b_value, sink_keys, sink_values = fetched[:-3]
    lengths, sink_count, window = fetched[-3:]
    pieces = [mine, others[0]]
    for far in others[1:]:
        pieces += [swap_kv(far, n_kv, 1), far]
    half = jax.ShapeDtypeStruct((rows // 2, wide), f32)
    keep, send = pl.pallas_call(
        lambda *refs: project_kernel(count, n_kv, *refs),
        out_shape=(half, half),
        in_specs=[spec()] * (n_kv + 4),
        out_specs=(spec(), spec()),
        compiler_params=pltpu.CompilerParams(vmem_limit_bytes=16 << 20),
        name="project",
    )(*pieces, gain, *weights)

    visits = cycle // BLOCK + 1

    def load(cache, plan, turn, name):
        loaded = (count, heads_kv, visits * BLOCK, size)
        turned = (count, heads_kv * size, visits * BLOCK)
        sem = pltpu.SemaphoreType.DMA((count, visits))
        kernel = load_cache_kernel
        if not turn:
            kernel = lambda plan, cache, out, sem: load_cache_kernel(plan, cache, out, None, sem)
        return pl.pallas_call(
            kernel,
            out_shape=jax.ShapeDtypeStruct(turned if turn else loaded, bf16),
            in_specs=[spec(), spec(pltpu.HBM)],
            out_specs=spec(),
            scratch_shapes=([pltpu.VMEM(loaded, bf16)] if turn else []) + [sem],
            compiler_params=pltpu.CompilerParams(vmem_limit_bytes=(12 if turn else 1) << 20),
            cost_estimate=pl.CostEstimate(flops=0, transcendentals=0, bytes_accessed=6 << 20),
            name=name,
        )(plan, in_hbm(cache))

    req_stages = stages(n_req)
    plan = plan_of(lengths, sink_count, window)
    keep, plan = lax.optimization_barrier((keep, plan))
    received = swap_req(send, n_req, n_kv, req_stages[0][1])
    k_live = load(key_cache, plan, True, "load_keys")
    keep, k_live = lax.optimization_barrier((keep, k_live))
    parts = [keep, received]
    for radix, unit in req_stages[1:]:
        x = sum(parts[1:], parts[0])
        chunk = x.shape[0] // radix
        parts = [x[:chunk]] + [
            swap_req(x[q * chunk : (q + 1) * chunk], n_req, n_kv, q * unit)
            for q in range(1, radix)
        ]
    parts[0], plan = lax.optimization_barrier((parts[0], plan))
    v_live = load(value_cache, plan, False, "load_values")

    freq = jnp.power(1000000.0, -2.0 * jnp.arange(size // 2, dtype=f32) / size)
    angle = lengths.astype(f32)[:, None] * freq
    cos, sin = jnp.cos(angle), jnp.sin(angle)
    cosine = jnp.concatenate([cos, cos], 1)
    sine = jnp.concatenate([-sin, sin], 1)

    context = attend_call(
        plan, parts, cosine, sine, b_query, b_key, b_value, k_live, v_live, sink_keys, sink_values
    )

    everyone = context
    for radix, unit in stages(n_req):
        blocks = [swap_req(everyone, n_req, n_kv, q * unit) for q in range(1, radix)]
        everyone = jnp.concatenate([everyone] + blocks, 0)
    piece = jax.ShapeDtypeStruct((rows_kv, w_output.shape[1]), f32)
    products = pl.pallas_call(
        output_kernel,
        out_shape=(piece,) * n_kv,
        in_specs=[spec()] * 2,
        out_specs=(spec(),) * n_kv,
        compiler_params=pltpu.CompilerParams(vmem_limit_bytes=16 << 20),
        name="output",
    )(everyone, w_output)
    result = products[0]
    for u in range(n_kv - 1, 0, -1):
        result = result + swap_kv(products[u], n_kv, u)
    return result.astype(bf16)


def solution(mesh):
    in_specs = (
        P("kv", "req"),
        P("req"),
        P("req", "kv"),
        P("req", "kv"),
        P("req", "kv"),
        P("kv"),
        P("kv"),
        P("kv"),
        P("kv", "req"),
        P("req", "kv", None, None),
        P("req", "kv", None, None),
        P("req", "kv", None, None),
        P("req", "kv", None, None),
        P("req"),
        P("req"),
        P("req"),
    )
    out_specs = P("kv", "req")
    return jax.shard_map(
        on_device, mesh=mesh, in_specs=in_specs, out_specs=out_specs, check_vma=False
    )
```

```python
import functools
import math

import jax
import jax.numpy as jnp
from jax import lax
from jax.experimental import pallas as pl
from jax.experimental.pallas import tpu as pltpu
from jax.sharding import PartitionSpec as P

D = 5120
SINKS = 4
EPS = 1e-06
BLOCK = 512
PLAN_BITS = 4
TOGETHER = 16
STEP = 2
LANES = 128
FAR = 1 << 20
EXTRA_ROWS = 16


def log2(n):
    bits = n.bit_length() - 1
    assert n == 1 << bits
    return bits


def stages(n):
    bits = log2(n)
    if bits == 0:
        return []
    result = [(2, 1)]
    left = bits - 1
    while left:
        take = 2 if left % 2 == 0 else 1
        left -= take
        result.append((1 << take, 2 << left))
    return result


def crossed(offset, kv):
    low = offset & 3
    turned = ((low & 1) << 1) | (low >> 1)
    return offset ^ ((low ^ turned) * (kv & 1))


def place_to_offset(place, n, gathered):
    offset = place * 0
    for radix, unit in stages(n) if gathered else reversed(stages(n)):
        offset = offset + (place & (radix - 1)) * unit
        place = place >> log2(radix)
    return offset


def swap_req(x, n_req, n_kv, offset):
    pairs = [
        (i * n_kv + j, (i ^ (crossed(offset, j) if n_req > 2 else offset)) * n_kv + j)
        for i in range(n_req)
        for j in range(n_kv)
    ]
    return lax.ppermute(x, ("req", "kv"), pairs)


def swap_kv(x, n_kv, offset):
    return lax.ppermute(x, "kv", [(j, j ^ offset) for j in range(n_kv)])


def row_order(size, rows_req, rows_kv, to_kv):
    req, kv = lax.axis_index("req"), lax.axis_index("kv")
    n_req = size // rows_req
    shape = (size, size)
    req_row = lax.broadcasted_iota(jnp.int32, shape, 1 if to_kv else 0)
    kv_row = lax.broadcasted_iota(jnp.int32, shape, 0 if to_kv else 1)
    offset = place_to_offset(req_row >> log2(rows_req), n_req, to_kv)
    if n_req > 2:
        offset = crossed(offset, kv)
    request = ((offset ^ req) << log2(rows_req)) | (req_row & (rows_req - 1))
    kv_request = (((request >> log2(rows_kv)) ^ kv) << log2(rows_kv)) | (request & (rows_kv - 1))
    return (kv_request == kv_row).astype(jnp.bfloat16)


def prepare_kernel(rows_req, rows_kv, n, sink_keys, sink_values, *refs):
    sources, copied = refs[:n], refs[n : 2 * n]
    order_in, order_out, k_extra, v_extra, k_sinks, v_sinks, sem = refs[2 * n :]
    pairs = list(zip(sources, copied)) + [(sink_keys, k_sinks), (sink_values, v_sinks)]
    copies = [
        pltpu.make_async_copy(source, target, sem.at[i]) for i, (source, target) in enumerate(pairs)
    ]
    for copy in copies:
        copy.start()
    size = order_in.shape[0]
    order_in[...] = row_order(size, rows_req, rows_kv, False)
    order_out[...] = row_order(size, rows_req, rows_kv, True)
    k_extra[...] = jnp.zeros_like(k_extra)
    v_extra[...] = jnp.zeros_like(v_extra)
    for copy in copies:
        copy.wait()
    for r in range(k_sinks.shape[0]):
        for h in range(k_sinks.shape[1]):
            lanes = slice(h * k_sinks.shape[3], (h + 1) * k_sinks.shape[3])
            k_extra[r, 0:SINKS, lanes] = k_sinks[r, h].astype(jnp.float32)
            v_extra[r, 0:SINKS, lanes] = v_sinks[r, h].astype(jnp.float32)


def project_kernel(n_kv, *refs):
    pieces, (order, gain, w_query, w_key, w_value, keep, send) = refs[:n_kv], refs[n_kv:]
    hidden = jnp.concatenate([piece[...].astype(jnp.float32) for piece in pieces], 0)
    xf = jnp.dot(order[...], hidden.astype(jnp.bfloat16), preferred_element_type=jnp.float32)
    rows = gain[...].astype(jnp.float32)
    wide_gain = jnp.concatenate([rows[i : i + 1] for i in range(rows.shape[0])], 1)
    scaled = (xf * wide_gain).astype(jnp.bfloat16)
    half = keep.shape[0]

    def put(start, block):
        width = block.shape[1]
        keep[:, start : start + width] = block[:half]
        send[:, start : start + width] = block[half:]

    at = 0
    for weight in (w_query, w_key, w_value):
        put(at, jnp.dot(scaled, weight[...], preferred_element_type=jnp.float32))
        at += weight.shape[1]
    squares = jnp.sum(xf * xf, 1, keepdims=True)
    put(at, jnp.broadcast_to(squares, (2 * half, LANES)))


def plan_of(lengths, sink_count, window):
    count = lengths.shape[0]
    low = jnp.maximum(sink_count, lengths - window)
    first = low // BLOCK
    visits = (lengths - 1) // BLOCK - first + 1
    shift = PLAN_BITS * 2 * jnp.arange(count, dtype=jnp.int32)
    plan = jnp.stack(
        [
            low - first * BLOCK,
            lengths - first * BLOCK,
            jnp.minimum(sink_count, lengths),
            (first | (visits << PLAN_BITS)) << shift,
        ]
    )
    return jnp.broadcast_to(plan[:, :, None], (4, count, LANES))


def visits_of(plan, count):
    mask = (1 << PLAN_BITS) - 1
    packed = sum(plan[3, r : r + 1] for r in range(count))[0, 0]
    fields = [
        lax.shift_right_logical(packed, jnp.int32(PLAN_BITS * i)) & mask for i in range(2 * count)
    ]
    return list(zip(fields[::2], fields[1::2]))


def load_cache_kernel(plan, cache, out, buf, sem):
    count, heads_kv, cycle, size = cache.shape
    planned = visits_of(plan, count)
    target = out if buf is None else buf

    def each(act):
        for r, (first, visits) in enumerate(planned):

            @pl.loop(0, visits)
            def _(t):
                at = (first + t) & (cycle // BLOCK - 1)
                src = pl.ds(pl.multiple_of(at * BLOCK, BLOCK), BLOCK)
                dst = pl.ds(pl.multiple_of(t * BLOCK, BLOCK), BLOCK)
                copy = pltpu.make_async_copy(
                    cache.at[r, :, src], target.at[r, :, dst], sem.at[r, t]
                )
                act(copy, r, dst)

    def finish(copy, r, slots):
        copy.wait()
        if buf is not None:
            for h in range(heads_kv):
                out[r, h * size : (h + 1) * size, slots] = buf[r, h, slots].T

    each(lambda copy, r, slots: copy.start())
    each(finish)


def attend_kernel(n_parts, plan, *refs):
    parts = refs[:n_parts]
    (
        cosine,
        sine,
        b_query,
        b_key,
        b_value,
        k_buf,
        v_buf,
        k_extra,
        v_extra,
        context,
        score_buf,
        q_heads,
        result_buf,
        q_rows,
        tops,
        denoms,
        numers,
    ) = refs[n_parts:]
    count, heads_kv, _, size = v_buf.shape
    q_cols, kv_cols = context.shape[1], heads_kv * size
    group = q_cols // kv_cols
    pad = q_heads.shape[1] // heads_kv
    scale = 1.0 / math.sqrt(size)
    planned = visits_of(plan, count)

    total = parts[0][...]
    for part in parts[1:]:
        total = total + part[...]
    columns = q_cols + 2 * kv_cols
    inv_rms = lax.rsqrt(total[:, columns : columns + 1] / D + EPS)
    bias = jnp.concatenate([b[...].astype(jnp.float32) for b in (b_query, b_key, b_value)], 0)

    def head_of(i):
        return inv_rms * total[:, i * size : (i + 1) * size] + bias[i : i + 1]

    cos, sin = cosine[...], sine[...]

    def rotated(x):
        return x * cos + pltpu.roll(x, size // 2, 1) * sin

    q_heads[...] = jnp.zeros_like(q_heads)
    k_new, v_new = [], []
    for h in range(heads_kv):
        lanes = slice(h * size, (h + 1) * size)
        for g in range(group):
            head = h * group + g
            block = rotated(head_of(head))
            for r in range(count):
                q_heads[r, h * pad + g : h * pad + g + 1, lanes] = block[r : r + 1]
        k_new.append(rotated(head_of(heads_kv * group + h)))
        v_new.append(head_of(heads_kv * group + heads_kv + h))
    k_new, v_new = jnp.concatenate(k_new, 1), jnp.concatenate(v_new, 1)
    own_row = lax.broadcasted_iota(jnp.int32, (EXTRA_ROWS, 1), 0) == SINKS

    def extra_rows(base, new, r):
        return jnp.where(own_row, new[r : r + 1], base[r]).astype(jnp.bfloat16)

    contract_last = (((1,), (1,)), ((), ()))
    lane = lax.broadcasted_iota(jnp.int32, (1, EXTRA_ROWS), 1)
    offset = lax.broadcasted_iota(jnp.int32, (1, BLOCK), 1)
    repeats = BLOCK // LANES
    q_rows[...] = q_heads[...].astype(jnp.bfloat16)

    def both(buf, r, t):
        rows = pl.ds(pl.multiple_of(t * BLOCK, BLOCK), BLOCK)
        return jnp.concatenate([buf[r, h, rows] for h in range(heads_kv)], 1)

    def fold(x, op):
        pieces = [x[:, i : i + LANES] for i in range(0, x.shape[1], LANES)]
        while len(pieces) > 1:
            pieces = [op(*pieces[i : i + 2]) for i in range(0, len(pieces), 2)]
        return pieces[0]

    def score(r, t, place, at):
        s = (
            jnp.dot(
                q_rows[r],
                k_buf[r, :, pl.ds(pl.multiple_of(t * BLOCK, BLOCK), BLOCK)],
                preferred_element_type=jnp.float32,
            )
            * scale
        )
        position = at + offset
        low, high = (
            jnp.concatenate([plan[i, pl.ds(r, 1)]] * repeats, 1) for i in range(2)
        )
        s = jnp.where((position >= low) & (position < high), s, -jnp.inf)
        score_buf[place] = s
        return fold(s, jnp.maximum)

    def mix(r, t, place):
        weights = jnp.exp(score_buf[place] - jnp.concatenate([tops[r]] * repeats, 1))
        product = jnp.dot(
            weights.astype(jnp.bfloat16), both(v_buf, r, t), preferred_element_type=jnp.float32
        )
        return fold(weights, jnp.add), product

    starts = [0]
    for _, visits in planned:
        starts.append(starts[-1] + visits - 1)
    left = starts[-1]

    def block_of(place):
        inside = jnp.minimum(place, left - 1)
        r, start = 0, 0
        for i in range(1, count):
            past = inside >= starts[i]
            r = jnp.where(past, i, r)
            start = jnp.where(past, starts[i], start)
        return r, inside - start + 1

    rounds = left >> log2(TOGETHER)
    rest = left & (TOGETHER - 1)
    extras = []
    for r in range(count):
        extra = (
            lax.dot_general(
                q_rows[r],
                extra_rows(k_extra, k_new, r),
                contract_last,
                preferred_element_type=jnp.float32,
            )
            * scale
        )
        live = (lane < plan[2, r : r + 1, :EXTRA_ROWS]) | (lane == SINKS)
        extras.append(jnp.where(live, extra, -jnp.inf))
        tops[r] = score(r, 0, r, 0)

    def score_some(start, number):
        for i in range(number):
            place = start + i
            r, t = block_of(place)
            at = jnp.where(place < left, t * BLOCK, FAR)
            tops[r] = jnp.maximum(tops[r], score(r, t, count + place, at))

    def mix_some(start, number):
        for i in range(number):
            place = start + i
            r, t = block_of(place)
            denom, product = mix(r, t, count + place)
            denoms[r] += denom
            numers[r] += product

    def all_others(some):
        pl.loop(0, rounds)(lambda k: some(k * TOGETHER, TOGETHER))
        for size in range(STEP, TOGETHER + 1, STEP):
            fits = (rest > size - STEP) & (rest <= size)
            pl.when(fits)(functools.partial(some, rounds * TOGETHER, size))

    all_others(score_some)
    for r in range(count):
        top = jnp.maximum(
            jnp.max(tops[r], 1, keepdims=True), jnp.max(extras[r], 1, keepdims=True)
        )
        tops[r] = jnp.broadcast_to(top, tops.shape[1:])
        extras[r] = jnp.exp(extras[r] - top)
        numer = jnp.dot(
            extras[r].astype(jnp.bfloat16),
            extra_rows(v_extra, v_new, r),
            preferred_element_type=jnp.float32,
        )
        denoms[r], product = mix(r, 0, r)
        numers[r] = numer + product

    all_others(mix_some)

    for r in range(count):
        denom = jnp.sum(denoms[r], 1, keepdims=True) + jnp.sum(extras[r], 1, keepdims=True)
        result = numers[r] / denom
        for h in range(heads_kv):
            for g in range(group):
                head = h * group + g
                result_buf[r : r + 1, head * size : (head + 1) * size] = result[
                    h * pad + g : h * pad + g + 1, h * size : (h + 1) * size
                ]
    context[...] = result_buf[...].astype(context.dtype)


def output_kernel(n_pieces, order, w_output, *refs):
    pieces, outs = refs[:n_pieces], refs[n_pieces:]
    rows_kv = outs[0].shape[0]
    context = jnp.concatenate([piece[...].astype(jnp.float32) for piece in pieces], 0)
    context = context.astype(jnp.bfloat16)
    rows = jnp.dot(order[...], context, preferred_element_type=jnp.float32).astype(jnp.bfloat16)
    product = jnp.dot(rows, w_output[...], preferred_element_type=jnp.float32)
    for i, out in enumerate(outs):
        out[...] = product[i * rows_kv : (i + 1) * rows_kv]


def spec(space=pltpu.VMEM):
    return pl.BlockSpec(memory_space=space)


def attend_call(plan, parts, cosine, sine, b_query, b_key, b_value, k_live, v_live, *extras):
    count, heads_kv, stored, size = v_live.shape
    group = b_query.shape[0] // heads_kv
    rows, kv_cols = heads_kv * (-(-group // 8) * 8), heads_kv * size
    q_cols = b_query.shape[0] * size
    args = (plan, *parts, cosine, sine, b_query, b_key, b_value, k_live, v_live, *extras)
    return pl.pallas_call(
        lambda *refs: attend_kernel(len(parts), *refs),
        out_shape=jax.ShapeDtypeStruct((count, q_cols), jnp.bfloat16),
        in_specs=[spec()] * len(args),
        out_specs=spec(),
        scratch_shapes=[
            pltpu.VMEM((count * (stored // BLOCK) + TOGETHER, rows, BLOCK), jnp.float32),
            pltpu.VMEM((count, rows, kv_cols), jnp.float32),
            pltpu.VMEM((count, q_cols), jnp.float32),
            pltpu.VMEM((count, rows, kv_cols), jnp.bfloat16),
            pltpu.VMEM((count, rows, LANES), jnp.float32),
            pltpu.VMEM((count, rows, LANES), jnp.float32),
            pltpu.VMEM((count, rows, kv_cols), jnp.float32),
        ],
        compiler_params=pltpu.CompilerParams(vmem_limit_bytes=8 << 20),
        name="attend",
    )(*args)


def in_hbm(x):
    return pltpu.with_memory_space_constraint(x, pltpu.HBM)


def on_device(
    hidden,
    gain,
    w_query,
    w_key,
    w_value,
    b_query,
    b_key,
    b_value,
    w_output,
    key_cache,
    value_cache,
    sink_keys,
    sink_values,
    lengths,
    sink_count,
    window,
):
    n_req, n_kv = lax.axis_size("req"), lax.axis_size("kv")
    count, heads_kv, cycle, size = key_cache.shape
    rows_kv = hidden.shape[0]
    rows = count * n_req
    q_cols, kv_cols = w_query.shape[1], w_key.shape[1]
    wide = q_cols + 2 * kv_cols + LANES
    f32, bf16 = jnp.float32, jnp.bfloat16

    others = [swap_kv(hidden, n_kv, u) for u in range(1, n_kv, 2)]
    chunk = LANES if gain.shape[0] % LANES == 0 else gain.shape[0]
    wanted = (
        w_query,
        w_key,
        w_value,
        hidden,
        gain.reshape(-1, chunk),
        b_query.reshape(-1, size),
        b_key.reshape(-1, size),
        b_value.reshape(-1, size),
        lengths,
        sink_count,
        window,
    )
    square = jax.ShapeDtypeStruct((rows, rows), bf16)
    extra = jax.ShapeDtypeStruct((count, EXTRA_ROWS, kv_cols), f32)
    outs = [jax.ShapeDtypeStruct(w.shape, w.dtype) for w in wanted] + [square] * 2 + [extra] * 2
    n = len(wanted)
    fetched = pl.pallas_call(
        lambda *refs: prepare_kernel(count, rows_kv, n, *refs),
        out_shape=tuple(outs),
        in_specs=[spec(pltpu.HBM)] * (n + 2),
        out_specs=(spec(),) * len(outs),
        scratch_shapes=[
            pltpu.VMEM(sink_keys.shape, bf16),
            pltpu.VMEM(sink_values.shape, bf16),
            pltpu.SemaphoreType.DMA((n + 2,)),
        ],
        compiler_params=pltpu.CompilerParams(vmem_limit_bytes=2 << 20),
        cost_estimate=pl.CostEstimate(flops=0, transcendentals=0, bytes_accessed=6 << 20),
        name="prepare",
    )(*[in_hbm(w) for w in (sink_keys, sink_values, *wanted)])
    *weights, mine, gain, b_query, b_key, b_value = fetched[: n - 3]
    lengths, sink_count, window = fetched[n - 3 : n]
    order_in, order_out, *extras = fetched[n:]
    pieces = [mine, others[0]]
    for far in others[1:]:
        pieces += [swap_kv(far, n_kv, 1), far]
    half = jax.ShapeDtypeStruct((rows // 2, wide), f32)
    keep, send = pl.pallas_call(
        lambda *refs: project_kernel(n_kv, *refs),
        out_shape=(half, half),
        in_specs=[spec()] * (n_kv + 5),
        out_specs=(spec(), spec()),
        compiler_params=pltpu.CompilerParams(vmem_limit_bytes=16 << 20),
        name="project",
    )(*pieces, order_in, gain, *weights)

    visits = cycle // BLOCK + 1

    def load(cache, plan, turn, name):
        loaded = (count, heads_kv, visits * BLOCK, size)
        turned = (count, heads_kv * size, visits * BLOCK)
        sem = pltpu.SemaphoreType.DMA((count, visits))
        kernel = load_cache_kernel
        if not turn:
            kernel = lambda plan, cache, out, sem: load_cache_kernel(plan, cache, out, None, sem)
        return pl.pallas_call(
            kernel,
            out_shape=jax.ShapeDtypeStruct(turned if turn else loaded, bf16),
            in_specs=[spec(), spec(pltpu.HBM)],
            out_specs=spec(),
            scratch_shapes=([pltpu.VMEM(loaded, bf16)] if turn else []) + [sem],
            compiler_params=pltpu.CompilerParams(vmem_limit_bytes=(12 if turn else 1) << 20),
            cost_estimate=pl.CostEstimate(flops=0, transcendentals=0, bytes_accessed=6 << 20),
            name=name,
        )(plan, in_hbm(cache))

    req_stages = stages(n_req)
    plan = plan_of(lengths, sink_count, window)
    keep, plan = lax.optimization_barrier((keep, plan))
    received = swap_req(send, n_req, n_kv, req_stages[0][1])
    k_live = load(key_cache, plan, True, "load_keys")
    keep, k_live = lax.optimization_barrier((keep, k_live))
    parts = [keep, received]
    for radix, unit in req_stages[1:]:
        x = sum(parts[1:], parts[0])
        chunk = x.shape[0] // radix
        parts = [x[:chunk]] + [
            swap_req(x[q * chunk : (q + 1) * chunk], n_req, n_kv, q * unit)
            for q in range(1, radix)
        ]
    parts[0], plan = lax.optimization_barrier((parts[0], plan))
    v_live = load(value_cache, plan, False, "load_values")

    freq = jnp.power(1000000.0, -2.0 * jnp.arange(size // 2, dtype=f32) / size)
    angle = lengths.astype(f32)[:, None] * freq
    cos, sin = jnp.cos(angle), jnp.sin(angle)
    cosine = jnp.concatenate([cos, cos], 1)
    sine = jnp.concatenate([-sin, sin], 1)

    context = attend_call(
        plan, parts, cosine, sine, b_query, b_key, b_value, k_live, v_live, *extras
    )

    pieces = [context]
    for radix, unit in stages(n_req):
        everyone = jnp.concatenate(pieces, 0) if len(pieces) > 1 else pieces[0]
        blocks = [swap_req(everyone, n_req, n_kv, q * unit) for q in range(1, radix)]
        pieces = [everyone] + blocks
    piece = jax.ShapeDtypeStruct((rows_kv, w_output.shape[1]), f32)
    products = pl.pallas_call(
        lambda *refs: output_kernel(len(pieces), *refs),
        out_shape=(piece,) * n_kv,
        in_specs=[spec()] * (len(pieces) + 2),
        out_specs=(spec(),) * n_kv,
        compiler_params=pltpu.CompilerParams(vmem_limit_bytes=16 << 20),
        name="output",
    )(order_out, w_output, *pieces)
    result = products[0]
    for u in range(n_kv - 1, 0, -1):
        result = result + swap_kv(products[u], n_kv, u)
    return result.astype(bf16)


def solution(mesh):
    in_specs = (
        P("kv", "req"),
        P("req"),
        P("req", "kv"),
        P("req", "kv"),
        P("req", "kv"),
        P("kv"),
        P("kv"),
        P("kv"),
        P("kv", "req"),
        P("req", "kv", None, None),
        P("req", "kv", None, None),
        P("req", "kv", None, None),
        P("req", "kv", None, None),
        P("req"),
        P("req"),
        P("req"),
    )
    out_specs = P("kv", "req")
    return jax.shard_map(
        on_device, mesh=mesh, in_specs=in_specs, out_specs=out_specs, check_vma=False
    )
```
